32 devices in a mesh: outer: 16 (over z, x, core), inner: 2 (over y).
Axes of the slice: x: 2, y: 2, z: 4, core: 2. Of those that a mesh axis runs over, the one named last changes fastest.
Arguments:
- qkv: bfloat16 [2048, 8, 10, 128], P(('outer', 'inner')), may hold values from -96 to 96
- key_codes: int32 [2048, 8, 16], P('outer', 'inner'), may hold values from 0 to 255
- codebooks: bfloat16 [8, 256, 128], P('inner'), may hold values from -4 to 4
- value_codes: bfloat16 [2048, 8, 128], P('outer', 'inner'), may hold values from -4 to 4
- value_scales: float32 [2048, 8], P('outer', 'inner'), may hold values from 0.25 to 4
- block_ids: int32 [16], P('outer'), may hold values from 0 to 15, each once
Outputs:
- attended: bfloat16 [2048, 8, 8, 128], P(('outer', 'inner'))
The draws below stay inside these ranges and needn't reach their ends.
All inputs are finite; a program needn't handle non-finite values.
Results may differ from the reference program's by a relative error of at most 0.011.
Values may be sent and summed in bfloat16 or wider, within the bound.
No kernel may reach another device: no remote copies, remote signals or barrier semaphores. Data moves between devices by JAX's collectives and lax.ppermute only.
A program may use at most 64 MiB of HBM per device.

```python
import math
import jax
import jax.numpy as jnp
from jax import lax

KV = 8
HEAD = 128
CODES = 256
BLOCK = 128
GQ = 8
GROUPS = 16
STRETCH = 128
TOKENS = 2048
PREFIX = 2048
N_OUTER = 16


def draw_qkv(key, part):
    key_query, key_key, key_value = jax.random.split(jax.random.fold_in(key, 7), 3)
    query_shape = (TOKENS, KV, GQ, HEAD)
    single_shape = (TOKENS, KV, 1, HEAD)
    queries = 2.5 * jax.random.truncated_normal(key_query, -4.0, 4.0, query_shape, jnp.float32)
    keys_new = jax.random.truncated_normal(key_key, -4.0, 4.0, single_shape, jnp.float32)
    values_new = jax.random.truncated_normal(key_value, -4.0, 4.0, single_shape, jnp.float32)
    return jnp.concatenate([queries, keys_new, values_new], axis=2).astype(jnp.bfloat16)


def touch_ends(result, rng, least, top_value):
    longest = result.shape.index(max(result.shape))
    spots = []
    for shift in (0, 1):
        where = [jax.random.randint(jax.random.fold_in(rng, axis), (), 0, length) for axis, length in enumerate(result.shape)]
        where[longest] = (where[longest] + shift) % result.shape[longest]
        spots.append(tuple(where))
    return result.at[spots[0]].set(least).at[spots[1]].set(top_value)


def level_of(key, shape, cuts, low, largest):
    gain = 1.0
    for dim, shards_of in cuts:
        draws = jax.random.uniform(jax.random.fold_in(jax.random.fold_in(key, 6), dim), (shards_of,), jnp.float32, low / len(cuts), largest / len(cuts))
        gain = gain * jnp.repeat(jnp.exp(draws), shape[dim] // shards_of).reshape((-1,) + (1,) * (len(shape) - 1 - dim))
    return gain


def bell_draw(key, shape, spread, bound, cuts=(), kind=jnp.bfloat16):
    array = jax.random.normal(key, shape, jnp.float32) * spread
    if len(cuts) > 0:
        array = level_of(key, shape, cuts, -0.22, 0.18) * array
    return jnp.clip(array, min=-bound, max=bound).astype(kind)


def setup_inputs(seed: int = 0) -> dict:
    streams_of = jax.random.split(jax.random.key(seed), 7)
    qkv = draw_qkv(jax.random.fold_in(streams_of[6], 71), 0)
    key_codes = touch_ends(jax.random.randint(streams_of[1], (PREFIX, KV, GROUPS), 0, CODES), jax.random.fold_in(streams_of[1], 1), 0, CODES - 1).astype(jnp.int32)
    codebooks = bell_draw(streams_of[2], (KV, CODES, HEAD), 1.0, 4.0, ((0, 2),))
    value_codes = bell_draw(streams_of[3], (PREFIX, KV, HEAD), 1.0, 4.0, ((0, 16), (1, 2)))
    value_scales = jnp.clip(jnp.exp(math.log(4.0) - 2.7725887 * jax.random.uniform(streams_of[4], (PREFIX, KV), jnp.float32) ** level_of(streams_of[4], (PREFIX, KV), ((0, 16), (1, 2)), -0.2, 0.2)), 0.25, 4.0)
    block_ids = jax.random.permutation(streams_of[5], N_OUTER).astype(jnp.int32)
    return dict(qkv=qkv, key_codes=key_codes, codebooks=codebooks, value_codes=value_codes, value_scales=value_scales, block_ids=block_ids)


rope_base = 500000.0


def rotate(tensor, position):
    half_dim = tensor.shape[-1] // 2
    ladder = jnp.arange(half_dim, dtype=jnp.float32)
    inverse = jnp.exp(ladder * jnp.float32(-2.0 * math.log(rope_base) / tensor.shape[-1]))
    angles = position.astype(jnp.float32)[:, None] * inverse[None, :]
    target = (position.shape[0],) + (1,) * (tensor.ndim - 2) + (half_dim,)
    cosine = jnp.cos(angles).reshape(target)
    sine_part = jnp.sin(angles).reshape(target)
    floats = tensor.astype(jnp.float32)
    first_half = floats[..., :half_dim]
    second_half = floats[..., half_dim:]
    return jnp.concatenate([first_half * cosine - second_half * sine_part, second_half * cosine + first_half * sine_part], axis=-1)


def reference(qkv, key_codes, codebooks, value_codes, value_scales, block_ids):
    code_table = codebooks.reshape(KV, CODES, GROUPS, 8)
    picked = code_table[jnp.arange(KV, dtype=jnp.int32)[None, :, None], key_codes, jnp.arange(GROUPS, dtype=jnp.int32)[None, None, :]]
    raw_keys = picked.reshape(PREFIX, KV, HEAD)
    prefix_rows = jnp.arange(PREFIX, dtype=jnp.int32)
    prefix_pos = block_ids[prefix_rows // BLOCK] * BLOCK + prefix_rows % BLOCK
    prefix_keys = rotate(raw_keys, prefix_pos).astype(jnp.bfloat16)
    prefix_values = (value_codes.astype(jnp.float32) * value_scales[:, :, None]).astype(jnp.bfloat16)
    tokens = jnp.arange(TOKENS, dtype=jnp.int32)
    stretch_pos = PREFIX + tokens % STRETCH
    queries = rotate(qkv[:, :, :GQ, :], stretch_pos).astype(jnp.bfloat16)
    stretch_keys = rotate(qkv[:, :, GQ, :], stretch_pos).astype(jnp.bfloat16)
    stretch_values = qkv[:, :, GQ + 1, :]
    local_pos = jnp.arange(STRETCH, dtype=jnp.int32)
    allowed = jnp.concatenate([jnp.ones((STRETCH, PREFIX), dtype=bool), local_pos[None, :] <= local_pos[:, None]], axis=1)
    score_scale = HEAD ** -0.5

    def attend_group(pair_index):
        stretch_index = pair_index // KV
        kv_index = pair_index % KV
        first_row = (stretch_index * STRETCH).astype(jnp.int32)
        query_rows = lax.dynamic_index_in_dim(lax.dynamic_slice_in_dim(queries, first_row, STRETCH, 0), kv_index, 1, False)
        own_keys = lax.dynamic_index_in_dim(lax.dynamic_slice_in_dim(stretch_keys, first_row, STRETCH, 0), kv_index, 1, False)
        own_values = lax.dynamic_index_in_dim(lax.dynamic_slice_in_dim(stretch_values, first_row, STRETCH, 0), kv_index, 1, False)
        key_rows = jnp.concatenate([lax.dynamic_index_in_dim(prefix_keys, kv_index, 1, False), own_keys], axis=0)
        value_rows = jnp.concatenate([lax.dynamic_index_in_dim(prefix_values, kv_index, 1, False), own_values], axis=0)
        scores = jnp.einsum("tqd,nd->tqn", query_rows.astype(jnp.float32), key_rows.astype(jnp.float32)) * score_scale
        scores = jnp.where(allowed[:, None, :], scores, -jnp.inf)
        row_max = jnp.max(scores, axis=-1, keepdims=True)
        weights = jnp.exp(scores - row_max)
        weight_sum = jnp.sum(weights, axis=-1, keepdims=True)
        rounded = lax.optimization_barrier(weights.astype(jnp.bfloat16))
        mixed_rows = jnp.einsum("tqn,nd->tqd", rounded.astype(jnp.float32), value_rows.astype(jnp.float32))
        return (mixed_rows / weight_sum).astype(jnp.bfloat16)

    stacked = lax.map(attend_group, jnp.arange(N_OUTER * KV, dtype=jnp.int32))
    stacked = stacked.reshape(N_OUTER, KV, STRETCH, GQ, HEAD).transpose(0, 2, 1, 3, 4)
    return stacked.reshape(TOKENS, KV, GQ, HEAD)
```

```python
import functools
import math

import jax
import jax.numpy as jnp
import numpy as np
from jax import lax
from jax.experimental import pallas as pl
from jax.experimental.pallas import tpu as pltpu
from jax.sharding import PartitionSpec as P

rope_base = 500000.0
axes = ("outer", "inner")
bf16 = jnp.bfloat16
f32 = jnp.float32


def frequencies(head_dim):
    ladder = np.arange(head_dim // 2, dtype=np.float32)
    return np.exp(ladder * np.float32(-2.0 * math.log(rope_base) / head_dim)).astype(np.float32)


def angle_table(positions, head_dim):
    return frequencies(head_dim)[:, None] * positions.astype(np.float32)[None, :]


def whole(memory=pltpu.VMEM):
    return pl.BlockSpec(memory_space=memory)


def params(megabytes=48):
    return pltpu.CompilerParams(vmem_limit_bytes=megabytes * 2**20)


def pack_prefix(place, ids, codes, values, scales, half):
    rows, kv_local, groups = codes.shape
    head_dim = values.shape[-1]
    extent = half * (rows + groups)

    def kernel(place, ids, codes, values, scales, keep, send):
        core = place[0]
        block = jnp.full((16, head_dim), ids[0], jnp.int32).astype(f32).astype(bf16)
        lane = lax.broadcasted_iota(jnp.int32, scales.shape, 1)
        factors = scales[...]
        for target, which in ((send, 1 - core), (keep, core)):
            for k in range(half):
                head = which * half + k
                factor = jnp.sum(jnp.where(lane == head, factors, 0.0), axis=1, keepdims=True)
                target[k * rows : (k + 1) * rows, :] = (values[head].astype(f32) * factor).astype(bf16)
                first = half * rows + k * groups
                target[first : first + groups, :] = codes[head].astype(f32).astype(bf16)
        send[extent:, :] = block

    return pl.pallas_call(
        kernel,
        out_shape=(
            jax.ShapeDtypeStruct((extent, head_dim), bf16),
            jax.ShapeDtypeStruct((extent + 16, head_dim), bf16),
        ),
        in_specs=[whole(pltpu.SMEM), whole(pltpu.SMEM), whole(), whole(), whole()],
        out_specs=(whole(), whole()),
        compiler_params=params(),
        name="pack_prefix",
    )(place, ids, codes.transpose(1, 2, 0), values.transpose(1, 0, 2), scales)


def rotate_stretch(heads, cosine, sine, qkv, half_heads):
    tokens, _, slots, head_dim = qkv.shape
    group = slots - 2
    rows = tokens * group + 2 * tokens

    def kernel(heads, cosine, sine, qkv, keep, send):
        step = pl.program_id(0)
        cos, sin = cosine[...], sine[...]
        q = qkv[:, 0, :group, :].astype(f32)
        turned = q * cos[:, None, :] + pltpu.roll(q, head_dim // 2, 2) * sin[:, None, :]
        turned = turned.reshape(tokens * group, head_dim).astype(bf16)
        key = qkv[:, 0, group, :].astype(f32)
        key = (key * cos + pltpu.roll(key, head_dim // 2, 1) * sin).astype(bf16)
        value = qkv[:, 0, group + 1, :]

        def put(target):
            target[0, : tokens * group, :] = turned
            target[0, tokens * group : tokens * (group + 1), :] = key
            target[0, tokens * (group + 1) :, :] = value

        @pl.when(step < half_heads)
        def _():
            put(send)

        @pl.when(step >= half_heads)
        def _():
            put(keep)

    shape = jax.ShapeDtypeStruct((half_heads, rows, head_dim), bf16)
    return pl.pallas_call(
        kernel,
        out_shape=(shape, shape),
        grid_spec=pltpu.PrefetchScalarGridSpec(
            num_scalar_prefetch=1,
            grid=(2 * half_heads,),
            in_specs=[
                pl.BlockSpec((tokens, head_dim), lambda i, h: (0, 0)),
                pl.BlockSpec((tokens, head_dim), lambda i, h: (0, 0)),
                pl.BlockSpec((tokens, 1, slots, head_dim), lambda i, h: (0, h[i], 0, 0)),
            ],
            out_specs=[
                pl.BlockSpec((1, rows, head_dim), lambda i, h: (jnp.maximum(i - half_heads, 0), 0, 0)),
                pl.BlockSpec((1, rows, head_dim), lambda i, h: (jnp.minimum(i, half_heads - 1), 0, 0)),
            ],
        ),
        compiler_params=params(),
        name="rotate_stretch",
    )(heads, cosine, sine, qkv)


def attend(place, pieces, tables, book, queries, stretch, state, heads, sizes, final):
    half, rows, groups, tokens, group, head_dim, codes = sizes
    n_blocks = sum(len(blocks) for _, blocks in pieces)
    length = n_blocks * rows
    q_rows = tokens * group
    all_rows = 2 * q_rows
    tile = min(256, q_rows)
    scale = head_dim**-0.5 * math.log2(math.e)
    n_pieces = len(pieces)
    gd = head_dim // groups
    half_dim = head_dim // 2
    book_array, book_start = book

    operands = [a for a, _ in pieces] + list(tables) + [book_array, queries[0], queries[1]]
    if stretch is not None:
        operands.append(stretch[0])
    n_plain = len(operands) + 1
    if state is not None:
        operands += list(state)

    def kernel(place, *refs):
        refs = list(refs)
        piece_refs = [refs.pop(0) for _ in range(n_pieces)]
        cos_tok, sin_tok, cos_blk, sin_blk = [refs.pop(0) for _ in range(4)]
        book_ref, q0, q1 = [refs.pop(0) for _ in range(3)]
        other = refs.pop(0) if stretch is not None else None
        before = [refs.pop(0) for _ in range(3)] if state is not None else None
        if final:
            outs = refs.pop(0)
            after = None
        else:
            after = [refs.pop(0) for _ in range(3)]
        kt, vv, tab = [refs.pop(0) for _ in range(3)]
        core, inner = place[0], place[1]

        for k in range(half):
            if book_start is None:
                entries = book_ref[core * half + k]
            else:
                entries = book_ref[book_start + k * codes : book_start + (k + 1) * codes, :]
            tab[k] = entries.astype(f32).T

        index = 0
        for ref, (_, blocks) in zip(piece_refs, pieces):
            for value_row, code_row, id_row in blocks:
                block = ref[id_row - id_row % 16 : id_row - id_row % 16 + 16, :].astype(f32)
                block = block[id_row % 16 : id_row % 16 + 8].astype(jnp.int32)
                block = jnp.broadcast_to(block[None], (half_dim // 8, 8, head_dim)).reshape(half_dim, head_dim)
                cb = jnp.take_along_axis(cos_blk[...], block, axis=1, mode="promise_in_bounds")
                sb = jnp.take_along_axis(sin_blk[...], block, axis=1, mode="promise_in_bounds")
                ct, st = cos_tok[...], sin_tok[...]
                cos = cb * ct - sb * st
                sin = sb * ct + cb * st
                for k in range(half):
                    code = ref[code_row + k * groups : code_row + (k + 1) * groups, :].astype(f32).astype(jnp.int32)
                    code = jnp.broadcast_to(code[:, None, :], (groups, gd, rows)).reshape(head_dim, rows)
                    low = code & 127
                    key = jnp.take_along_axis(tab[k, :, :128], low, axis=1, mode="promise_in_bounds")
                    for part in range(1, codes // 128):
                        more = jnp.take_along_axis(tab[k, :, part * 128 : (part + 1) * 128], low, axis=1, mode="promise_in_bounds")
                        key = jnp.where(code >= part * 128, more, key)
                    a, b = key[:half_dim], key[half_dim:]
                    key = jnp.concatenate([a * cos - b * sin, b * cos + a * sin], axis=0).astype(bf16)
                    span = slice(index * rows, (index + 1) * rows)
                    kt[k, :head_dim, span] = key
                    kt[k, head_dim:, span] = key
                    vv[k, span, :] = ref[value_row + k * rows : value_row + (k + 1) * rows, :]
                index += 1

        def soft(score, m, l, total, value):
            new_m = jnp.maximum(m, jnp.max(score, axis=1, keepdims=True))
            weight = jnp.exp2(score - new_m)
            part = weight[:, :128]
            for i in range(1, weight.shape[1] // 128):
                part = part + weight[:, i * 128 : (i + 1) * 128]
            mixed = jnp.dot(weight.astype(bf16), value, preferred_element_type=f32)
            if m is None:
                return new_m, part, mixed
            decay = jnp.exp2(m - new_m)
            return new_m, l * decay + part, total * decay + mixed

        per_head = q_rows // tile

        def body(which, query, i):
            k = i // per_head
            rr = pl.multiple_of((i % per_head) * tile, tile)
            out_row = pl.multiple_of(which * q_rows + rr, tile)
            hk = heads[0] + k
            q = query[hk, pl.ds(rr, tile), :]
            scaled = q.astype(f32) * scale
            hi = scaled.astype(bf16)
            lo = (scaled - hi.astype(f32)).astype(bf16)
            q = jnp.concatenate([hi, lo], axis=1)
            if before is not None:
                at = (k, pl.ds(out_row, tile), slice(None))
                m, l, total = before[0][at][:, :1], before[1][at], before[2][at]
            else:
                m = jnp.full((tile, 1), -1e30, f32)
                l = jnp.zeros((tile, 128), f32)
                total = jnp.zeros((tile, head_dim), f32)
            score = jnp.dot(q, kt[k], preferred_element_type=f32)
            m, l, total = soft(score, m, l, total, vv[k])
            if stretch is not None:
                first, per = stretch[1], 2 * tokens
                mate = (heads[0] + half) % (2 * half)
                base = pl.multiple_of(first + (which * 2 * half + mate + k) * per, 2 * tokens)
                key_other = other[pl.ds(base, tokens), :]
                value_other = other[pl.ds(base + tokens, tokens), :]
                key_own = query[hk, q_rows : q_rows + tokens, :]
                value_own = query[hk, q_rows + tokens :, :]
                key = jnp.concatenate([key_other, key_own], axis=0)
                key = jnp.concatenate([key, key], axis=1)
                value = jnp.concatenate([value_other, value_own], axis=0)
                score = lax.dot_general(q, key, (((1,), (1,)), ((), ())), preferred_element_type=f32)
                column = lax.broadcasted_iota(jnp.int32, score.shape, 1)
                row = (lax.broadcasted_iota(jnp.int32, score.shape, 0) + rr) // group
                allowed = (column - tokens <= row) & (column >= tokens * (1 - inner))
                score = jnp.where(allowed, score, -jnp.inf)
                m, l, total = soft(score, m, l, total, value)
            at = (k, pl.ds(out_row, tile), slice(None))
            if final:
                denominator = jnp.sum(l, axis=1, keepdims=True)
                outs[at] = (total / denominator).astype(bf16)
            else:
                after[0][at] = jnp.broadcast_to(m, (tile, 128))
                after[1][at] = l
                after[2][at] = total

        for which, query in enumerate((q0, q1)):

            @pl.loop(0, half * per_head)
            def _(i, which=which, query=query):
                body(which, query, i)

    wide = jax.ShapeDtypeStruct((half, all_rows, 128), f32)
    if final:
        out_shape = jax.ShapeDtypeStruct((half, all_rows, head_dim), bf16)
        out_specs = whole()
        alias = {}
    else:
        out_shape = (wide, wide, wide)
        out_specs = (whole(),) * 3
        alias = {n_plain + j: j for j in range(3)} if state is not None else {}
    flops = 4 * half * all_rows * length * head_dim
    return pl.pallas_call(
        kernel,
        out_shape=out_shape,
        in_specs=[whole(pltpu.SMEM)] + [whole() for _ in operands],
        out_specs=out_specs,
        scratch_shapes=[
            pltpu.VMEM((half, 2 * head_dim, length), bf16),
            pltpu.VMEM((half, length, head_dim), bf16),
            pltpu.VMEM((half, head_dim, codes), f32),
        ],
        input_output_aliases=alias,
        compiler_params=params(),
        cost_estimate=pl.CostEstimate(
            flops=2 * flops, bytes_accessed=4 * 2**20, transcendentals=half * all_rows * length
        ),
        name="attend",
    )(place, *operands)


def lay_out(heads, own, received, tokens, group):
    arrays = [a for a, _ in own] + [a for a, _ in received]
    half = arrays[0].shape[0]
    head_dim = arrays[0].shape[2]
    n_heads = half * len(arrays)
    q_rows = tokens * group
    blocks = [b for _, b in own] + [b for _, b in received]

    def kernel(heads, *refs):
        step = pl.program_id(0)
        out = refs[-1]
        for j, ref in enumerate(refs[:-1]):

            @pl.when(step // half == j)
            def _(ref=ref):
                out[:, 0, :, :] = ref[0].reshape(tokens, group, head_dim)

    def pick(j, block):
        return lambda i, h: (jnp.clip(i - j * half, 0, half - 1), block, 0)

    return pl.pallas_call(
        kernel,
        out_shape=jax.ShapeDtypeStruct((tokens, n_heads, group, head_dim), bf16),
        grid_spec=pltpu.PrefetchScalarGridSpec(
            num_scalar_prefetch=1,
            grid=(n_heads,),
            in_specs=[pl.BlockSpec((1, q_rows, head_dim), pick(j, b)) for j, b in enumerate(blocks)],
            out_specs=pl.BlockSpec((tokens, 1, group, head_dim), lambda i, h: (0, h[i], 0, 0)),
        ),
        compiler_params=params(),
        name="lay_out",
    )(heads, *arrays)


def paired(qkv, key_codes, codebooks, value_codes, value_scales, block_ids, *, n_outer):
    tokens, n_heads, slots, head_dim = qkv.shape
    group = slots - 2
    rows, kv_local, groups = key_codes.shape
    codes = codebooks.shape[1]
    half = kv_local // 2
    n_far = n_outer // 4
    prefix = rows * n_outer
    outer, inner = lax.axis_index("outer"), lax.axis_index("inner")
    core = outer % 2
    place = jnp.stack([core, inner]).astype(jnp.int32)
    extent = half * (rows + groups)

    def swap(x, outer_bits, inner_bits=0):
        return lax.ppermute(
            x,
            axes,
            [
                (2 * o + i, 2 * (o ^ outer_bits) + (i ^ inner_bits))
                for o in range(n_outer)
                for i in range(2)
            ],
        )

    keep, send = pack_prefix(place, block_ids, key_codes, value_codes, value_scales, half)
    mate = swap(send, 1)

    own_first = jnp.stack([inner, 1 - inner]).astype(jnp.int32)

    def order(which):
        return (own_first[:, None] * kv_local + which * half + jnp.arange(half)[None, :]).reshape(-1).astype(jnp.int32)

    cosine = np.cos(angle_table(np.arange(2 * tokens) + prefix, head_dim)).T
    sine = np.sin(angle_table(np.arange(2 * tokens) + prefix, head_dim)).T
    cosine = jnp.asarray(np.concatenate([cosine, cosine], axis=1))
    sine = jnp.asarray(np.concatenate([-sine, sine], axis=1))
    cosine = lax.dynamic_slice_in_dim(cosine, inner * tokens, tokens, 0)
    sine = lax.dynamic_slice_in_dim(sine, inner * tokens, tokens, 0)
    q_keep, q_send = rotate_stretch(
        jnp.concatenate([order(1 - core), order(core)]), cosine, sine, qkv, 2 * half
    )
    q_mate = swap(q_send, 1)

    own_id = jnp.full((8, head_dim), block_ids[0].astype(bf16))
    pack = jnp.concatenate([keep, mate[:extent], own_id, mate[extent + 8 :]], axis=0)
    size = pack.shape[0]

    def blocks_of(base, count=1):
        out = []
        for j in range(count):
            b = base + j * size
            out.append((b, b + half * rows, b + 2 * extent))
            out.append((b + extent, b + extent + half * rows, b + 2 * extent + 8))
        return out

    def far(x):
        return [swap(x, 4 * j) for j in range(1, n_far)]

    z_packs = far(pack)
    diag = swap(pack, 2, 1)
    x_pack = swap(pack, 2)
    my_books = lax.dynamic_slice_in_dim(codebooks, core * half, half, 0).reshape(half * codes, head_dim)
    q_rows = tokens * group
    kv_own = jnp.concatenate([q_keep[:, q_rows:], q_mate[:, q_rows:]], axis=0).reshape(-1, head_dim)
    y_send = jnp.concatenate([pack, my_books, kv_own], axis=0)
    y_pack = swap(y_send, 0, 1)
    book_row = size
    stretch_row = size + half * codes

    z_all = jnp.concatenate(z_packs, axis=0)
    y_far = swap(z_all, 0, 1)
    diag_far = far(diag)
    x_far = swap(z_all, 2)

    positions = np.arange(rows)
    cos_tok, sin_tok = np.cos(angle_table(positions, head_dim)), np.sin(angle_table(positions, head_dim))
    starts = np.arange(128) * rows
    cos_blk, sin_blk = np.cos(angle_table(starts, head_dim)), np.sin(angle_table(starts, head_dim))
    tables = [jnp.asarray(t.astype(np.float32)) for t in (cos_tok, sin_tok, cos_blk, sin_blk)]
    sizes = (half, rows, groups, tokens, group, head_dim, codes)
    queries = (q_keep, q_mate)
    call = functools.partial(attend, place, tables=tables, queries=queries, sizes=sizes)

    one = blocks_of(0)
    many = blocks_of(0, n_far - 1)
    own_state = call(
        [(pack, one)] + [(p, one) for p in z_packs] + [(x_pack, one)],
        book=(codebooks, None), stretch=(y_pack, stretch_row), state=None, heads=(0,), final=False,
    )
    own_out = call([(x_far, many)], book=(codebooks, None), stretch=None, state=own_state, heads=(0,), final=True)
    own_mate = swap(own_out[:, q_rows:], 1)
    other_state = call(
        [(y_pack, one), (diag, one)] + [(p, one) for p in diag_far],
        book=(y_pack, book_row), stretch=(y_pack, stretch_row), state=None, heads=(half,), final=False,
    )
    other_out = call([(y_far, many)], book=(y_pack, book_row), stretch=None, state=other_state, heads=(half,), final=True)
    other_mate = swap(other_out[:, q_rows:], 1)
    return lay_out(
        jnp.concatenate([order(core), order(1 - core)]),
        [(own_out, 0), (other_out, 0)],
        [(own_mate, 0), (other_mate, 0)],
        tokens,
        group,
    )


def rotate(tensor, position):
    half_dim = tensor.shape[-1] // 2
    ladder = jnp.arange(half_dim, dtype=jnp.float32)
    inverse = jnp.exp(ladder * jnp.float32(-2.0 * math.log(rope_base) / tensor.shape[-1]))
    angles = position.astype(jnp.float32)[:, None] * inverse[None, :]
    target = (position.shape[0],) + (1,) * (tensor.ndim - 2) + (half_dim,)
    cosine = jnp.cos(angles).reshape(target)
    sine_part = jnp.sin(angles).reshape(target)
    floats = tensor.astype(jnp.float32)
    first_half = floats[..., :half_dim]
    second_half = floats[..., half_dim:]
    return jnp.concatenate(
        [
            first_half * cosine - second_half * sine_part,
            second_half * cosine + first_half * sine_part,
        ],
        axis=-1,
    )


def decode_block(key_codes, codebooks):
    block_rows, kv_local, group_count = key_codes.shape
    entries = codebooks.shape[1]
    head_dim = codebooks.shape[2]
    ladder = lax.broadcasted_iota(jnp.int32, (1, 1, 1, entries), 3).astype(jnp.float32)
    one_hot = (key_codes.astype(jnp.float32)[..., None] == ladder).astype(jnp.bfloat16)
    code_table = codebooks.reshape(kv_local, entries, group_count, head_dim // group_count)
    decoded = jnp.einsum("bkgc,kcgd->bkgd", one_hot, code_table, preferred_element_type=jnp.float32)
    return decoded.reshape(block_rows, kv_local, head_dim)


def span_of():
    return 1024


def absorb(state, queries, key_rows, value_rows, allowed):
    running_max, running_sum, weighted = state
    scores = jnp.einsum(
        "tkgd,nkd->tkgn", queries, key_rows, preferred_element_type=jnp.float32
    ) * queries.shape[-1] ** (-0.5)
    if allowed is not None:
        scores = jnp.where(allowed[:, None, None, :], scores, -jnp.inf)
    new_max = jnp.maximum(running_max, jnp.max(scores, axis=-1))
    decay_factor = jnp.exp(running_max - new_max)
    weights = jnp.exp(scores - new_max[..., None])
    running_sum = running_sum * decay_factor + jnp.sum(weights, axis=-1)
    weighted = weighted * decay_factor[..., None] + jnp.einsum(
        "tkgn,nkd->tkgd",
        weights.astype(jnp.bfloat16),
        value_rows,
        preferred_element_type=jnp.float32,
    )
    return (new_max, running_sum, weighted)


def shards(qkv, key_codes, codebooks, value_codes, value_scales, block_ids):
    group_heads = qkv.shape[2] - 2
    head_dim = qkv.shape[3]
    block_rows = key_codes.shape[0]
    prefix_len = block_rows * lax.axis_size("outer")
    prefix_values = (value_codes.astype(jnp.float32) * value_scales[:, :, None]).astype(
        jnp.bfloat16
    )
    exchanged = lax.all_to_all(qkv, "inner", split_axis=1, concat_axis=0, tiled=True)
    stretch_rows = exchanged.shape[0]
    kv_local = exchanged.shape[1]
    local_pos = jnp.arange(stretch_rows, dtype=jnp.int32)
    stretch_pos = prefix_len + local_pos
    queries = rotate(exchanged[:, :, :group_heads, :], stretch_pos).astype(jnp.bfloat16)
    stretch_keys = rotate(exchanged[:, :, group_heads, :], stretch_pos).astype(jnp.bfloat16)
    stretch_values = exchanged[:, :, group_heads + 1, :]
    initial = (
        jnp.full((stretch_rows, kv_local, group_heads), -1e30, jnp.float32),
        jnp.zeros((stretch_rows, kv_local, group_heads), jnp.float32),
        jnp.zeros((stretch_rows, kv_local, group_heads, head_dim), jnp.float32),
    )
    own_pos = block_ids[0] * block_rows + jnp.arange(block_rows, dtype=jnp.int32)
    prefix_keys = rotate(decode_block(key_codes, codebooks), own_pos).astype(jnp.bfloat16)
    key_rows = lax.all_gather(prefix_keys, "outer", axis=0, tiled=True)
    value_rows = lax.all_gather(prefix_values, "outer", axis=0, tiled=True)
    length = key_rows.shape[0]
    span_rows = span_of()

    def advance(step_index, inner_state):
        first_row = step_index * span_rows
        key_part = lax.dynamic_slice_in_dim(key_rows, first_row, span_rows, 0)
        value_part = lax.dynamic_slice_in_dim(value_rows, first_row, span_rows, 0)
        return absorb(inner_state, queries, key_part, value_part, None)

    allowed = local_pos[None, :] <= local_pos[:, None]
    final_state = lax.fori_loop(
        0,
        length // span_rows,
        advance,
        absorb(initial, queries, stretch_keys, stretch_values, allowed),
    )
    running_max, running_sum, weighted = final_state
    outputs = (weighted / running_sum[..., None]).astype(jnp.bfloat16)
    return lax.all_to_all(outputs, "inner", split_axis=0, concat_axis=1, tiled=True)


def solution(mesh):
    n_outer, n_inner = mesh.shape["outer"], mesh.shape["inner"]

    def body(qkv, key_codes, codebooks, value_codes, value_scales, block_ids):
        arrays = (qkv, key_codes, codebooks, value_codes, value_scales, block_ids)
        head_dim = qkv.shape[3]
        far = n_outer // 4
        fits = (
            n_inner == 2
            and n_outer % 4 == 0
            and 1 < far
            and far & (far - 1) == 0
            and n_outer <= 128
            and key_codes.shape[1] % 2 == 0
            and key_codes.shape[0] == 128
            and head_dim == 128
            and head_dim // key_codes.shape[2] == 8
            and key_codes.shape[2] % 16 == 0
            and codebooks.shape[1] % 128 == 0
            and qkv.shape[2] == 10
            and qkv.shape[0] % 32 == 0
        )
        if fits:
            return paired(*arrays, n_outer=n_outer)
        return shards(*arrays)

    return jax.shard_map(
        body,
        mesh=mesh,
        in_specs=(
            P(("outer", "inner"), None, None, None),
            P("outer", "inner", None),
            P("inner", None, None),
            P("outer", "inner", None),
            P("outer", "inner"),
            P("outer"),
        ),
        out_specs=P(("outer", "inner"), None, None, None),
        check_vma=False,
    )
```

```python
import functools
import math

import jax
import jax.numpy as jnp
import numpy as np
from jax import lax
from jax.experimental import pallas as pl
from jax.experimental.pallas import tpu as pltpu
from jax.sharding import PartitionSpec as P

rope_base = 500000.0
axes = ("outer", "inner")
bf16 = jnp.bfloat16
f32 = jnp.float32


def frequencies(head_dim):
    ladder = np.arange(head_dim // 2, dtype=np.float32)
    return np.exp(ladder * np.float32(-2.0 * math.log(rope_base) / head_dim)).astype(np.float32)


def angle_table(positions, head_dim):
    return frequencies(head_dim)[:, None] * positions.astype(np.float32)[None, :]


def whole(memory=pltpu.VMEM):
    return pl.BlockSpec(memory_space=memory)


def params(megabytes=16):
    return pltpu.CompilerParams(vmem_limit_bytes=megabytes * 2**20)


def pack_prefix(place, ids, codes, values, scales, half):
    rows, kv_local, groups = codes.shape
    head_dim = values.shape[-1]
    extent = half * (rows + groups)

    def kernel(place, ids, codes, values, scales, keep, send):
        core = place[0]
        diagonal = lax.broadcasted_iota(jnp.int32, (rows, rows), 0) == lax.broadcasted_iota(jnp.int32, (rows, rows), 1)

        def put(target, head, k):
            factor = jnp.broadcast_to(scales[head : head + 1, :], (rows, rows))
            factor = jnp.sum(jnp.where(diagonal, factor, 0.0), axis=1, keepdims=True)
            target[k * rows : (k + 1) * rows, :] = (values[:, head, :].astype(f32) * factor).astype(bf16)
            first = half * rows + k * groups
            target[first : first + groups, :] = codes[head].astype(f32).astype(bf16)

        for side in range(2):

            @pl.when(core == side)
            def _():
                for k in range(half):
                    put(send, (1 - side) * half + k, k)
                    put(keep, side * half + k, k)

        send[extent:, :] = jnp.full((16, head_dim), ids[0], jnp.int32).astype(f32).astype(bf16)

    return pl.pallas_call(
        kernel,
        out_shape=(
            jax.ShapeDtypeStruct((extent, head_dim), bf16),
            jax.ShapeDtypeStruct((extent + 16, head_dim), bf16),
        ),
        in_specs=[whole(pltpu.SMEM), whole(pltpu.SMEM), whole(), whole(), whole()],
        out_specs=(whole(), whole()),
        compiler_params=params(),
        name="pack_prefix",
    )(place, ids, codes.transpose(1, 2, 0), values, scales.T)


def rotate_stretch(heads, cosine, sine, qkv, half_heads):
    tokens, n_heads, slots, head_dim = qkv.shape
    group = slots - 2
    q_rows = tokens * group
    rows = q_rows + 2 * tokens

    def kernel(heads, cosine, sine, qkv, keep, send, q_scratch, k_scratch, v_scratch):
        cos, sin = cosine[...][:, None, :], sine[...][:, None, :]

        def turn(x):
            return x * cos + pltpu.roll(x, head_dim // 2, 2) * sin

        spread = (tokens, 1, n_heads, head_dim)
        for slot in range(group):
            x = turn(qkv[:, slot, :, :].astype(f32))
            q_scratch[:, slot : slot + 1, :, :] = x.reshape(spread)
        k_scratch[...] = turn(qkv[:, group, :, :].astype(f32))
        v_scratch[...] = qkv[:, group + 1, :, :].astype(f32)
        q_flat = q_scratch.reshape(q_rows * n_heads, head_dim)
        k_flat = k_scratch.reshape(tokens * n_heads, head_dim)
        v_flat = v_scratch.reshape(tokens * n_heads, head_dim)
        for step in range(2 * half_heads):
            target = send if step < half_heads else keep
            at = step % half_heads
            head = heads[step]
            target[at, :q_rows, :] = q_flat[pl.ds(head, q_rows, stride=n_heads), :].astype(bf16)
            target[at, q_rows : q_rows + tokens, :] = k_flat[pl.ds(head, tokens, stride=n_heads), :].astype(bf16)
            target[at, q_rows + tokens :, :] = v_flat[pl.ds(head, tokens, stride=n_heads), :].astype(bf16)

    shape = jax.ShapeDtypeStruct((half_heads, rows, head_dim), bf16)
    return pl.pallas_call(
        kernel,
        out_shape=(shape, shape),
        in_specs=[whole(pltpu.SMEM), whole(), whole(), whole()],
        out_specs=(whole(), whole()),
        scratch_shapes=[
            pltpu.VMEM((tokens, group, n_heads, head_dim), f32),
            pltpu.VMEM((tokens, n_heads, head_dim), f32),
            pltpu.VMEM((tokens, n_heads, head_dim), f32),
        ],
        compiler_params=params(),
        name="rotate_stretch",
    )(heads, cosine, sine, qkv.transpose(0, 2, 1, 3))


def attend(place, groups_of, tables, queries, stretch, state, sizes, final, megabytes=32):
    half, rows, groups, tokens, group, head_dim, codes = sizes
    q_rows = tokens * group
    scale = head_dim**-0.5 * math.log2(math.e)
    gd = head_dim // groups
    half_dim = head_dim // 2
    n_heads = queries[0].shape[0]
    lengths = [sum(len(blocks) for _, blocks in pieces) * rows for _, _, pieces, _ in groups_of]
    extra = 2 * tokens if stretch is not None else 0
    chunk = 768

    operands, where = [], {}

    def ref_of(array):
        if id(array) not in where:
            where[id(array)] = len(operands)
            operands.append(array)
        return where[id(array)]

    plan = [
        (first, ref_of(book), row, [(ref_of(array), blocks) for array, blocks in pieces])
        for first, (book, row), pieces, _ in groups_of
    ]
    table_at = [ref_of(t) for t in tables]
    query_at = [ref_of(q) for q in queries]
    stretch_at = ref_of(stretch) if stretch is not None else None
    n_plain = len(operands)
    if state is not None:
        operands += list(state)

    def kernel(place, *refs):
        refs = list(refs)
        given = refs[:n_plain]
        before = refs[n_plain : n_plain + 3] if state is not None else None
        refs = refs[len(operands) :]
        results = refs[: 2 if final else 3]
        refs = refs[len(results) :]
        kts, vvs = refs[: len(plan)], refs[len(plan) : 2 * len(plan)]
        tab, slots = refs[2 * len(plan)], refs[2 * len(plan) + 1 :]
        core, inner = place[0], place[1]
        cos_tok, sin_tok, cos_blk, sin_blk = [given[i] for i in table_at]
        requests = [given[i] for i in query_at]
        other = given[stretch_at] if stretch is not None else None

        def decode(group_index):
            first, book_at, book_row, pieces = plan[group_index]
            kt, vv, book = kts[group_index], vvs[group_index], given[book_at]
            for k in range(half):
                if book_row is None:
                    entries = book[core * half + k]
                else:
                    entries = book[book_row + k * codes : book_row + (k + 1) * codes, :]
                tab[k] = entries.astype(f32).T
            index = 0
            for at, blocks in pieces:
                ref = given[at]
                for value_row, code_row, id_row in blocks:
                    base = id_row - id_row % 16
                    block = ref[base : base + 16, :].astype(f32)
                    block = block[id_row % 16 : id_row % 16 + 8].astype(jnp.int32)
                    block = jnp.broadcast_to(block[None], (half_dim // 8, 8, head_dim)).reshape(half_dim, head_dim)
                    cb = jnp.take_along_axis(cos_blk[...], block, axis=1, mode="promise_in_bounds")
                    sb = jnp.take_along_axis(sin_blk[...], block, axis=1, mode="promise_in_bounds")
                    ct, st = cos_tok[...], sin_tok[...]
                    cos = cb * ct - sb * st
                    sin = sb * ct + cb * st
                    span = slice(index * rows, (index + 1) * rows)
                    for k in range(half):
                        code = ref[code_row + k * groups : code_row + (k + 1) * groups, :].astype(f32).astype(jnp.int32)
                        code = jnp.broadcast_to(code[:, None, :], (groups, gd, rows)).reshape(head_dim, rows)
                        low = code & 127
                        key = jnp.take_along_axis(tab[k, :, :128], low, axis=1, mode="promise_in_bounds")
                        for part in range(1, codes // 128):
                            entries = tab[k, :, part * 128 : (part + 1) * 128]
                            more = jnp.take_along_axis(entries, low, axis=1, mode="promise_in_bounds")
                            key = jnp.where(code >= part * 128, more, key)
                        a, b = key[:half_dim], key[half_dim:]
                        key = jnp.concatenate([a * cos - b * sin, b * cos + a * sin], axis=0).astype(bf16)
                        kt[k, :head_dim, span] = key
                        kt[k, head_dim:, span] = key
                        vv[k, span, :] = ref[value_row + k * rows : value_row + (k + 1) * rows, :]
                    index += 1

        for group_index in range(len(plan)):
            decode(group_index)

        works = [(g, k, e) for g in range(len(plan)) for k in range(half) for e in range(2)]

        def parts(work):
            return [(c, min(chunk, lengths[work[0]] - c)) for c in range(0, lengths[work[0]], chunk)]

        def prepare(work):
            g, k, e = work
            scaled = requests[e][plan[g][0] + k, :q_rows, :].astype(f32) * scale
            hi = scaled.astype(bf16)
            lo = (scaled - hi.astype(f32)).astype(bf16)
            return jnp.concatenate([hi, lo], axis=1)

        def fold(top, score):
            for i in range(score.shape[1] // 128):
                piece = score[:, i * 128 : (i + 1) * 128]
                top = piece if top is None else jnp.maximum(top, piece)
            return top

        def score_part(work, q, slot, top, c, width):
            score = jnp.dot(q, kts[work[0]][work[1], :, c : c + width], preferred_element_type=f32)
            slot[:, c : c + width] = score
            return fold(top, score)

        def stretch_rows(work, which):
            g, k, e = work
            head = plan[g][0] + k
            base = (e * n_heads + (head + half) % n_heads) * 2 * tokens + which * tokens
            mine = q_rows + which * tokens
            return jnp.concatenate([other[base : base + tokens, :], requests[e][head, mine : mine + tokens, :]], axis=0)

        def score_stretch(work, q, slot, top):
            key = stretch_rows(work, 0)
            key = jnp.concatenate([key, key], axis=1)
            score = lax.dot_general(q, key, (((1,), (1,)), ((), ())), preferred_element_type=f32)
            column = lax.broadcasted_iota(jnp.int32, score.shape, 1)
            row = lax.broadcasted_iota(jnp.int32, score.shape, 0) // group
            allowed = (column - tokens <= row) & (column >= tokens * (1 - inner))
            score = jnp.where(allowed, score, -jnp.inf)
            slot[:, lengths[work[0]] : lengths[work[0]] + extra] = score
            return fold(top, score)

        def weigh(slot, m, part, mixed, c, width, value):
            weights = []
            for i in range(c, c + width, 128):
                weight = jnp.exp2(slot[:, i : i + 128] - m)
                part = part + weight
                weights.append(weight.astype(bf16))
            weight = jnp.concatenate(weights, axis=1) if len(weights) > 1 else weights[0]
            return part, mixed + jnp.dot(weight, value, preferred_element_type=f32)

        def place_of(work):
            g, k, e = work
            return plan[g][0] + k, slice(e * q_rows, (e + 1) * q_rows), slice(None)

        current = None
        for t in range(len(works) + 1):
            slot, old = slots[t % 2], slots[1 - t % 2]
            work = works[t] if t < len(works) else None
            top = None
            if work is not None:
                q = prepare(work)
            if current is not None:
                done, m, part, mixed = current
            if stretch is not None:
                if work is not None:
                    top = score_stretch(work, q, slot, top)
                if current is not None:
                    part, mixed = weigh(old, m, part, mixed, lengths[done[0]], extra, stretch_rows(done, 1))
            ahead = parts(work) if work is not None else []
            behind = parts(done) if current is not None else []
            for i in range(max(len(ahead), len(behind))):
                if i < len(ahead):
                    top = score_part(work, q, slot, top, *ahead[i])
                if i < len(behind):
                    c, width = behind[i]
                    part, mixed = weigh(old, m, part, mixed, c, width, vvs[done[0]][done[1], c : c + width, :])
            if current is not None:
                if final:
                    head = plan[done[0]][0] + done[1]
                    results[done[2]][head] = (mixed / jnp.sum(part, axis=1, keepdims=True)).astype(bf16)
                else:
                    for ref, value in zip(results, (m, part, mixed)):
                        ref[place_of(done)] = value
            if work is not None:
                m = jnp.broadcast_to(jnp.max(top, axis=1, keepdims=True), (q_rows, 128))
                if not groups_of[work[0]][3]:
                    part = jnp.zeros((q_rows, 128), f32)
                    mixed = jnp.zeros((q_rows, head_dim), f32)
                else:
                    past = before[0][place_of(work)]
                    m = jnp.maximum(past, m)
                    decay = jnp.exp2(past - m)
                    part = before[1][place_of(work)] * decay
                    mixed = before[2][place_of(work)] * decay
                current = (work, m, part, mixed)

    if final:
        out_shape = (jax.ShapeDtypeStruct((n_heads, q_rows, head_dim), bf16),) * 2
    else:
        out_shape = (jax.ShapeDtypeStruct((n_heads, 2 * q_rows, 128), f32),) * 3
    alias = {1 + n_plain + j: j for j in range(3)} if state is not None and not final else {}
    pairs = 2 * half * q_rows * (sum(lengths) + extra * len(plan))
    slot = pltpu.VMEM((q_rows, max(lengths) + extra), f32)
    return pl.pallas_call(
        kernel,
        out_shape=out_shape,
        in_specs=[whole(pltpu.SMEM)] + [whole() for _ in operands],
        out_specs=(whole(),) * len(out_shape),
        scratch_shapes=[pltpu.VMEM((half, 2 * head_dim, n), bf16) for n in lengths]
        + [pltpu.VMEM((half, n, head_dim), bf16) for n in lengths]
        + [pltpu.VMEM((half, head_dim, codes), f32), slot, slot],
        input_output_aliases=alias,
        compiler_params=params(megabytes),
        cost_estimate=pl.CostEstimate(flops=8 * pairs * head_dim, bytes_accessed=4 * 2**20, transcendentals=pairs),
        name="attend",
    )(place, *operands)


def lay_out(heads, own, received, tokens, group):
    arrays = list(own) + list(received)
    half, _, head_dim = arrays[0].shape
    q_rows = tokens * group

    def kernel(heads, *refs):
        out = refs[-1]
        for j, ref in enumerate(refs[:-1]):
            for k in range(half):
                out[:, pl.ds(heads[j * half + k], 1), :, :] = ref[k, :q_rows, :].reshape(tokens, 1, group, head_dim)

    return pl.pallas_call(
        kernel,
        out_shape=jax.ShapeDtypeStruct((tokens, half * len(arrays), group, head_dim), bf16),
        in_specs=[whole(pltpu.SMEM)] + [whole()] * len(arrays),
        out_specs=whole(),
        compiler_params=params(),
        name="lay_out",
    )(heads, *arrays)


def paired(qkv, key_codes, codebooks, value_codes, value_scales, block_ids, *, n_outer):
    tokens, n_heads, slots, head_dim = qkv.shape
    group = slots - 2
    rows, kv_local, groups = key_codes.shape
    codes = codebooks.shape[1]
    half = kv_local // 2
    n_far = n_outer // 4
    prefix = rows * n_outer
    outer, inner = lax.axis_index("outer"), lax.axis_index("inner")
    core = outer % 2
    place = jnp.stack([core, inner]).astype(jnp.int32)
    extent = half * (rows + groups)

    def swap(x, outer_bits, inner_bits=0):
        return lax.ppermute(
            x,
            axes,
            [
                (2 * o + i, 2 * (o ^ outer_bits) + (i ^ inner_bits))
                for o in range(n_outer)
                for i in range(2)
            ],
        )

    keep, send = pack_prefix(place, block_ids, key_codes, value_codes, value_scales, half)
    mate = swap(send, 1)

    own_id = jnp.full((8, head_dim), block_ids[0].astype(bf16))
    pack = jnp.concatenate([keep, mate[:extent], own_id, mate[extent + 8 :]], axis=0)
    size = pack.shape[0]

    def blocks_of(base, count=1):
        out = []
        for j in range(count):
            b = base + j * size
            out.append((b, b + half * rows, b + 2 * extent))
            out.append((b + extent, b + extent + half * rows, b + 2 * extent + 8))
        return out

    def along(parts, bits):
        return swap(jnp.concatenate(parts, axis=0) if len(parts) > 1 else parts[0], 4 * bits)

    my_books = lax.dynamic_slice_in_dim(codebooks, core * half, half, 0).reshape(half * codes, head_dim)
    z_far = [along([pack], n_far // 2)]
    diag = swap(pack, 2, 1)
    x_pack = swap(pack, 2)
    y_pack = swap(jnp.concatenate([pack, my_books], axis=0), 0, 1)
    z_far[0], diag, x_pack = lax.optimization_barrier((z_far[0], diag, x_pack))
    diag_far = [along([diag], n_far // 2)]
    bits = n_far // 4
    while bits:
        z_far.append(along([pack] + z_far, bits))
        bits //= 2

    mate, qkv = lax.optimization_barrier((mate, qkv))
    own_first = jnp.stack([inner, 1 - inner]).astype(jnp.int32)

    def order(which):
        return (own_first[:, None] * kv_local + which * half + jnp.arange(half)[None, :]).reshape(-1).astype(jnp.int32)

    cosine = np.cos(angle_table(np.arange(2 * tokens) + prefix, head_dim)).T
    sine = np.sin(angle_table(np.arange(2 * tokens) + prefix, head_dim)).T
    cosine = jnp.asarray(np.concatenate([cosine, cosine], axis=1))
    sine = jnp.asarray(np.concatenate([-sine, sine], axis=1))
    cosine = lax.dynamic_slice_in_dim(cosine, inner * tokens, tokens, 0)
    sine = lax.dynamic_slice_in_dim(sine, inner * tokens, tokens, 0)
    q_keep, q_send = rotate_stretch(
        jnp.concatenate([order(1 - core), order(core)]), cosine, sine, qkv, 2 * half
    )
    q_mate = swap(q_send, 1)

    q_rows = tokens * group

    positions = np.arange(rows)
    cos_tok, sin_tok = np.cos(angle_table(positions, head_dim)), np.sin(angle_table(positions, head_dim))
    starts = np.arange(128) * rows
    cos_blk, sin_blk = np.cos(angle_table(starts, head_dim)), np.sin(angle_table(starts, head_dim))
    tables = [jnp.asarray(t.astype(np.float32)) for t in (cos_tok, sin_tok, cos_blk, sin_blk)]
    sizes = (half, rows, groups, tokens, group, head_dim, codes)
    queries = (q_keep, q_mate)
    call = functools.partial(attend, place, tables=tables, queries=queries, sizes=sizes)
    own_book = (codebooks, None)

    def pieces(*arrays):
        return [(a, blocks_of(0, a.shape[0] // size)) for a in arrays]

    state = call([(0, own_book, pieces(pack, x_pack, z_far[0]), False)], stretch=None, state=None, final=False)
    kv_own = jnp.concatenate([q_keep[:, q_rows:], q_mate[:, q_rows:]], axis=0).reshape(-1, head_dim)
    kv_own, y_pack, *state = lax.optimization_barrier((kv_own, y_pack, *state))
    kv_pair = swap(kv_own, 0, 1)
    other_book, y_near = (y_pack, size), [(y_pack, blocks_of(0))]
    z_all = jnp.concatenate(z_far, axis=0)
    y_far = swap(z_all, 0, 1)
    x_far = swap(z_all, 2)
    diag_far[0], kv_pair = lax.optimization_barrier((diag_far[0], kv_pair))
    bits = n_far // 4
    while bits:
        diag_far.append(along([diag] + diag_far, bits))
        bits //= 2
    state = call(
        [(0, own_book, pieces(*z_far[1:]), True), (half, other_book, y_near + pieces(diag, diag_far[0]), False)],
        stretch=kv_pair, state=state, final=False,
    )
    out, out_send = call(
        [(0, own_book, pieces(x_far), True), (half, other_book, pieces(*diag_far[1:], y_far), True)],
        stretch=None, state=state, final=True,
    )
    out_mate = swap(out_send, 1)
    return lay_out(
        jnp.concatenate([order(core), order(1 - core)]),
        [out],
        [out_mate],
        tokens,
        group,
    )


def rotate(tensor, position):
    half_dim = tensor.shape[-1] // 2
    ladder = jnp.arange(half_dim, dtype=jnp.float32)
    inverse = jnp.exp(ladder * jnp.float32(-2.0 * math.log(rope_base) / tensor.shape[-1]))
    angles = position.astype(jnp.float32)[:, None] * inverse[None, :]
    target = (position.shape[0],) + (1,) * (tensor.ndim - 2) + (half_dim,)
    cosine = jnp.cos(angles).reshape(target)
    sine_part = jnp.sin(angles).reshape(target)
    floats = tensor.astype(jnp.float32)
    first_half = floats[..., :half_dim]
    second_half = floats[..., half_dim:]
    return jnp.concatenate(
        [
            first_half * cosine - second_half * sine_part,
            second_half * cosine + first_half * sine_part,
        ],
        axis=-1,
    )


def decode_block(key_codes, codebooks):
    block_rows, kv_local, group_count = key_codes.shape
    entries = codebooks.shape[1]
    head_dim = codebooks.shape[2]
    ladder = lax.broadcasted_iota(jnp.int32, (1, 1, 1, entries), 3).astype(jnp.float32)
    one_hot = (key_codes.astype(jnp.float32)[..., None] == ladder).astype(jnp.bfloat16)
    code_table = codebooks.reshape(kv_local, entries, group_count, head_dim // group_count)
    decoded = jnp.einsum("bkgc,kcgd->bkgd", one_hot, code_table, preferred_element_type=jnp.float32)
    return decoded.reshape(block_rows, kv_local, head_dim)


def span_of():
    return 1024


def absorb(state, queries, key_rows, value_rows, allowed):
    running_max, running_sum, weighted = state
    scores = jnp.einsum(
        "tkgd,nkd->tkgn", queries, key_rows, preferred_element_type=jnp.float32
    ) * queries.shape[-1] ** (-0.5)
    if allowed is not None:
        scores = jnp.where(allowed[:, None, None, :], scores, -jnp.inf)
    new_max = jnp.maximum(running_max, jnp.max(scores, axis=-1))
    decay_factor = jnp.exp(running_max - new_max)
    weights = jnp.exp(scores - new_max[..., None])
    running_sum = running_sum * decay_factor + jnp.sum(weights, axis=-1)
    weighted = weighted * decay_factor[..., None] + jnp.einsum(
        "tkgn,nkd->tkgd",
        weights.astype(jnp.bfloat16),
        value_rows,
        preferred_element_type=jnp.float32,
    )
    return (new_max, running_sum, weighted)


def shards(qkv, key_codes, codebooks, value_codes, value_scales, block_ids):
    group_heads = qkv.shape[2] - 2
    head_dim = qkv.shape[3]
    block_rows = key_codes.shape[0]
    prefix_len = block_rows * lax.axis_size("outer")
    prefix_values = (value_codes.astype(jnp.float32) * value_scales[:, :, None]).astype(
        jnp.bfloat16
    )
    exchanged = lax.all_to_all(qkv, "inner", split_axis=1, concat_axis=0, tiled=True)
    stretch_rows = exchanged.shape[0]
    kv_local = exchanged.shape[1]
    local_pos = jnp.arange(stretch_rows, dtype=jnp.int32)
    stretch_pos = prefix_len + local_pos
    queries = rotate(exchanged[:, :, :group_heads, :], stretch_pos).astype(jnp.bfloat16)
    stretch_keys = rotate(exchanged[:, :, group_heads, :], stretch_pos).astype(jnp.bfloat16)
    stretch_values = exchanged[:, :, group_heads + 1, :]
    initial = (
        jnp.full((stretch_rows, kv_local, group_heads), -1e30, jnp.float32),
        jnp.zeros((stretch_rows, kv_local, group_heads), jnp.float32),
        jnp.zeros((stretch_rows, kv_local, group_heads, head_dim), jnp.float32),
    )
    own_pos = block_ids[0] * block_rows + jnp.arange(block_rows, dtype=jnp.int32)
    prefix_keys = rotate(decode_block(key_codes, codebooks), own_pos).astype(jnp.bfloat16)
    key_rows = lax.all_gather(prefix_keys, "outer", axis=0, tiled=True)
    value_rows = lax.all_gather(prefix_values, "outer", axis=0, tiled=True)
    length = key_rows.shape[0]
    span_rows = span_of()

    def advance(step_index, inner_state):
        first_row = step_index * span_rows
        key_part = lax.dynamic_slice_in_dim(key_rows, first_row, span_rows, 0)
        value_part = lax.dynamic_slice_in_dim(value_rows, first_row, span_rows, 0)
        return absorb(inner_state, queries, key_part, value_part, None)

    allowed = local_pos[None, :] <= local_pos[:, None]
    final_state = lax.fori_loop(
        0,
        length // span_rows,
        advance,
        absorb(initial, queries, stretch_keys, stretch_values, allowed),
    )
    running_max, running_sum, weighted = final_state
    outputs = (weighted / running_sum[..., None]).astype(jnp.bfloat16)
    return lax.all_to_all(outputs, "inner", split_axis=0, concat_axis=1, tiled=True)


def solution(mesh):
    n_outer, n_inner = mesh.shape["outer"], mesh.shape["inner"]

    def body(qkv, key_codes, codebooks, value_codes, value_scales, block_ids):
        arrays = (qkv, key_codes, codebooks, value_codes, value_scales, block_ids)
        head_dim = qkv.shape[3]
        far = n_outer // 4
        fits = (
            n_inner == 2
            and n_outer % 4 == 0
            and 1 < far
            and far & (far - 1) == 0
            and n_outer <= 128
            and key_codes.shape[1] % 2 == 0
            and key_codes.shape[0] == 128
            and head_dim == 128
            and head_dim // key_codes.shape[2] == 8
            and key_codes.shape[2] % 16 == 0
            and codebooks.shape[1] % 128 == 0
            and qkv.shape[2] == 10
            and qkv.shape[0] % 32 == 0
        )
        if fits:
            return paired(*arrays, n_outer=n_outer)
        return shards(*arrays)

    return jax.shard_map(
        body,
        mesh=mesh,
        in_specs=(
            P(("outer", "inner"), None, None, None),
            P("outer", "inner", None),
            P("inner", None, None),
            P("outer", "inner", None),
            P("outer", "inner"),
            P("outer"),
        ),
        out_specs=P(("outer", "inner"), None, None, None),
        check_vma=False,
    )
```

```python
import functools
import math

import jax
import jax.numpy as jnp
import numpy as np
from jax import lax
from jax.experimental import pallas as pl
from jax.experimental.pallas import tpu as pltpu
from jax.sharding import PartitionSpec as P

rope_base = 500000.0
axes = ("outer", "inner")
bf16 = jnp.bfloat16
f32 = jnp.float32


def frequencies(head_dim):
    ladder = np.arange(head_dim // 2, dtype=np.float32)
    return np.exp(ladder * np.float32(-2.0 * math.log(rope_base) / head_dim)).astype(np.float32)


def angle_table(positions, head_dim):
    return frequencies(head_dim)[:, None] * positions.astype(np.float32)[None, :]


def whole(memory=pltpu.VMEM):
    return pl.BlockSpec(memory_space=memory)


def params(megabytes=16):
    return pltpu.CompilerParams(vmem_limit_bytes=megabytes * 2**20)


def prepare(place, ids, codes, values, scales, qkv, prefix, half):
    rows, kv_local, groups = codes.shape
    tokens, n_heads, slots, head_dim = qkv.shape
    group = slots - 2
    q_rows = tokens * group
    extent = half * (rows + groups)
    n_out = 2 * half
    kv_at = extent + 16 + n_out * q_rows
    size = kv_at + n_out * 2 * tokens
    angles = angle_table(np.arange(2 * tokens) + prefix, head_dim)
    cosine, sine = np.cos(angles).T, np.sin(angles).T
    cosine = jnp.asarray(np.concatenate([cosine, cosine], axis=1).astype(np.float32))
    sine = jnp.asarray(np.concatenate([-sine, sine], axis=1).astype(np.float32))
    sources = (codes.transpose(1, 2, 0), values, scales.T, qkv.transpose(0, 2, 1, 3), cosine, sine)

    def kernel(place, ids, *refs):
        given, (keep, send), held = refs[:6], refs[6:8], refs[8:14]
        codes, values, scales, qkv, cosine, sine = held
        q_scratch, k_scratch, v_scratch, sems = refs[14:]
        core, inner = place[0], place[1]
        copies = [pltpu.make_async_copy(*pair, sems.at[i]) for i, pair in enumerate(zip(given, held))]
        for copy in copies:
            copy.start()
        for copy in copies[:3]:
            copy.wait()
        diagonal = lax.broadcasted_iota(jnp.int32, (rows, rows), 0) == lax.broadcasted_iota(jnp.int32, (rows, rows), 1)

        def put(target, head, k):
            factor = jnp.broadcast_to(scales[head : head + 1, :], (rows, rows))
            factor = jnp.sum(jnp.where(diagonal, factor, 0.0), axis=1, keepdims=True)
            target[k * rows : (k + 1) * rows, :] = (values[:, head, :].astype(f32) * factor).astype(bf16)
            first = half * rows + k * groups
            target[first : first + groups, :] = codes[head].astype(f32).astype(bf16)

        for side in range(2):

            @pl.when(core == side)
            def _():
                for k in range(half):
                    put(send, (1 - side) * half + k, k)
                    put(keep, side * half + k, k)

        number = jnp.full((16, head_dim), ids[0], jnp.int32).astype(f32).astype(bf16)
        send[extent : extent + 16, :] = number
        keep[extent : extent + 16, :] = number
        for copy in copies[3:]:
            copy.wait()
        at = pl.ds(pl.multiple_of(inner * tokens, tokens), tokens)
        cos, sin = cosine[at, :][:, None, :], sine[at, :][:, None, :]

        def turn(x):
            return x * cos + pltpu.roll(x, head_dim // 2, 2) * sin

        spread = (tokens, 1, n_heads, head_dim)
        for slot in range(group):
            x = turn(qkv[:, slot, :, :].astype(f32))
            q_scratch[:, slot : slot + 1, :, :] = x.reshape(spread)
        k_scratch[...] = turn(qkv[:, group, :, :].astype(f32))
        v_scratch[...] = qkv[:, group + 1, :, :].astype(f32)
        q_flat = q_scratch.reshape(q_rows * n_heads, head_dim)
        k_flat = k_scratch.reshape(tokens * n_heads, head_dim)
        v_flat = v_scratch.reshape(tokens * n_heads, head_dim)
        for target, which in ((send, 1 - core), (keep, core)):
            for j in range(n_out):
                head = (inner if j < half else 1 - inner) * kv_local + which * half + j % half
                first = extent + 16 + j * q_rows
                target[first : first + q_rows, :] = q_flat[pl.ds(head, q_rows, stride=n_heads), :].astype(bf16)
                first = kv_at + j * 2 * tokens
                target[first : first + tokens, :] = k_flat[pl.ds(head, tokens, stride=n_heads), :].astype(bf16)
                first += tokens
                target[first : first + tokens, :] = v_flat[pl.ds(head, tokens, stride=n_heads), :].astype(bf16)

    shape = jax.ShapeDtypeStruct((size, head_dim), bf16)
    return pl.pallas_call(
        kernel,
        out_shape=(shape, shape),
        in_specs=[whole(pltpu.SMEM)] * 2 + [whole(pltpu.HBM)] * 6,
        out_specs=(whole(), whole()),
        scratch_shapes=[pltpu.VMEM(x.shape, x.dtype) for x in sources]
        + [
            pltpu.VMEM((tokens, group, n_heads, head_dim), f32),
            pltpu.VMEM((tokens, n_heads, head_dim), f32),
            pltpu.VMEM((tokens, n_heads, head_dim), f32),
            pltpu.SemaphoreType.DMA((6,)),
        ],
        compiler_params=params(),
        name="prepare",
    )(place, ids, *[pltpu.with_memory_space_constraint(x, pltpu.HBM) for x in sources])


def attend(place, groups_of, tables, queries, stretch, state, sizes, final, megabytes=32):
    half, rows, groups, tokens, group, head_dim, codes = sizes
    q_rows = tokens * group
    scale = head_dim**-0.5 * math.log2(math.e)
    gd = head_dim // groups
    half_dim = head_dim // 2
    n_heads = 2 * half
    q_at = half * (rows + groups) + 16
    kv_at = q_at + n_heads * q_rows
    lengths = [sum(len(blocks) for _, blocks in pieces) * rows for _, _, pieces, _ in groups_of]
    extra = 2 * tokens if stretch is not None else 0
    chunk = 768

    operands, where = [], {}

    def ref_of(array):
        if id(array) not in where:
            where[id(array)] = len(operands)
            operands.append(array)
        return where[id(array)]

    plan = [
        (first, ref_of(book), row, [(ref_of(array), blocks) for array, blocks in pieces])
        for first, (book, row), pieces, _ in groups_of
    ]
    table_at = [ref_of(t) for t in tables]
    query_at = [ref_of(q) for q in queries]
    stretch_at = ref_of(stretch) if stretch is not None else None
    n_plain = len(operands)
    if state is not None:
        operands += list(state)

    def kernel(place, *refs):
        refs = list(refs)
        given = refs[:n_plain]
        before = refs[n_plain : n_plain + 3] if state is not None else None
        refs = refs[len(operands) :]
        results = refs[: 2 if final else 3]
        refs = refs[len(results) :]
        kts, vvs = refs[: len(plan)], refs[len(plan) : 2 * len(plan)]
        tab, slots = refs[2 * len(plan)], refs[2 * len(plan) + 1 :]
        core, inner = place[0], place[1]
        cos_tok, sin_tok, cos_blk, sin_blk = [given[i] for i in table_at]
        requests = [given[i] for i in query_at]
        other = given[stretch_at] if stretch is not None else None

        def decode(group_index):
            first, book_at, book_row, pieces = plan[group_index]
            kt, vv, book = kts[group_index], vvs[group_index], given[book_at]
            for k in range(half):
                if book_row is None:
                    entries = book[core * half + k]
                else:
                    entries = book[book_row + k * codes : book_row + (k + 1) * codes, :]
                tab[k] = entries.astype(f32).T
            index = 0
            for at, blocks in pieces:
                ref = given[at]
                for value_row, code_row, id_row in blocks:
                    base = id_row - id_row % 16
                    block = ref[base : base + 16, :].astype(f32)
                    block = block[id_row % 16 : id_row % 16 + 8].astype(jnp.int32)
                    block = jnp.broadcast_to(block[None], (half_dim // 8, 8, head_dim)).reshape(half_dim, head_dim)
                    cb = jnp.take_along_axis(cos_blk[...], block, axis=1, mode="promise_in_bounds")
                    sb = jnp.take_along_axis(sin_blk[...], block, axis=1, mode="promise_in_bounds")
                    ct, st = cos_tok[...], sin_tok[...]
                    cos = cb * ct - sb * st
                    sin = sb * ct + cb * st
                    span = slice(index * rows, (index + 1) * rows)
                    for k in range(half):
                        code = ref[code_row + k * groups : code_row + (k + 1) * groups, :].astype(f32).astype(jnp.int32)
                        code = jnp.broadcast_to(code[:, None, :], (groups, gd, rows)).reshape(head_dim, rows)
                        low = code & 127
                        key = jnp.take_along_axis(tab[k, :, :128], low, axis=1, mode="promise_in_bounds")
                        for part in range(1, codes // 128):
                            entries = tab[k, :, part * 128 : (part + 1) * 128]
                            more = jnp.take_along_axis(entries, low, axis=1, mode="promise_in_bounds")
                            key = jnp.where(code >= part * 128, more, key)
                        a, b = key[:half_dim], key[half_dim:]
                        key = jnp.concatenate([a * cos - b * sin, b * cos + a * sin], axis=0).astype(bf16)
                        kt[k, :head_dim, span] = key
                        kt[k, head_dim:, span] = key
                        vv[k, span, :] = ref[value_row + k * rows : value_row + (k + 1) * rows, :]
                    index += 1

        for group_index in range(len(plan)):
            decode(group_index)

        works = [(g, k, e) for g in range(len(plan)) for k in range(half) for e in range(2)]

        def parts(work):
            return [(c, min(chunk, lengths[work[0]] - c)) for c in range(0, lengths[work[0]], chunk)]

        def scaled_queries(work):
            g, k, e = work
            first = q_at + (plan[g][0] + k) * q_rows
            scaled = requests[e][first : first + q_rows, :].astype(f32) * scale
            hi = scaled.astype(bf16)
            lo = (scaled - hi.astype(f32)).astype(bf16)
            return jnp.concatenate([hi, lo], axis=1)

        def fold(top, score):
            for i in range(score.shape[1] // 128):
                piece = score[:, i * 128 : (i + 1) * 128]
                top = piece if top is None else jnp.maximum(top, piece)
            return top

        def score_part(work, q, slot, top, c, width):
            score = jnp.dot(q, kts[work[0]][work[1], :, c : c + width], preferred_element_type=f32)
            slot[:, c : c + width] = score
            return fold(top, score)

        def stretch_rows(work, which):
            g, k, e = work
            head = plan[g][0] + k
            base = (e * n_heads + (head + half) % n_heads) * 2 * tokens + which * tokens
            mine = kv_at + head * 2 * tokens + which * tokens
            return jnp.concatenate([other[base : base + tokens, :], requests[e][mine : mine + tokens, :]], axis=0)

        def score_stretch(work, q, slot, top):
            key = stretch_rows(work, 0)
            key = jnp.concatenate([key, key], axis=1)
            score = lax.dot_general(q, key, (((1,), (1,)), ((), ())), preferred_element_type=f32)
            column = lax.broadcasted_iota(jnp.int32, score.shape, 1)
            row = lax.broadcasted_iota(jnp.int32, score.shape, 0) // group
            allowed = (column - tokens <= row) & (column >= tokens * (1 - inner))
            score = jnp.where(allowed, score, -jnp.inf)
            slot[:, lengths[work[0]] : lengths[work[0]] + extra] = score
            return fold(top, score)

        def weigh(slot, m, part, mixed, c, width, value):
            weights = []
            for i in range(c, c + width, 128):
                weight = jnp.exp2(slot[:, i : i + 128] - m)
                part = part + weight
                weights.append(weight.astype(bf16))
            weight = jnp.concatenate(weights, axis=1) if len(weights) > 1 else weights[0]
            return part, mixed + jnp.dot(weight, value, preferred_element_type=f32)

        def place_of(work):
            g, k, e = work
            return plan[g][0] + k, slice(e * q_rows, (e + 1) * q_rows), slice(None)

        current = None
        for t in range(len(works) + 1):
            slot, old = slots[t % 2], slots[1 - t % 2]
            work = works[t] if t < len(works) else None
            top = None
            if work is not None:
                q = scaled_queries(work)
            if current is not None:
                done, m, part, mixed = current
            if stretch is not None:
                if work is not None:
                    top = score_stretch(work, q, slot, top)
                if current is not None:
                    part, mixed = weigh(old, m, part, mixed, lengths[done[0]], extra, stretch_rows(done, 1))
            ahead = parts(work) if work is not None else []
            behind = parts(done) if current is not None else []
            for i in range(max(len(ahead), len(behind))):
                if i < len(ahead):
                    top = score_part(work, q, slot, top, *ahead[i])
                if i < len(behind):
                    c, width = behind[i]
                    part, mixed = weigh(old, m, part, mixed, c, width, vvs[done[0]][done[1], c : c + width, :])
            if current is not None:
                if final:
                    head = plan[done[0]][0] + done[1]
                    result = mixed / jnp.sum(part, axis=1, keepdims=True)
                    results[done[2]][head] = result.reshape(tokens, group, head_dim).astype(bf16)
                else:
                    for ref, value in zip(results, (m, part, mixed)):
                        ref[place_of(done)] = value
            if work is not None:
                m = jnp.broadcast_to(jnp.max(top, axis=1, keepdims=True), (q_rows, 128))
                if not groups_of[work[0]][3]:
                    part = jnp.zeros((q_rows, 128), f32)
                    mixed = jnp.zeros((q_rows, head_dim), f32)
                else:
                    past = before[0][place_of(work)]
                    m = jnp.maximum(past, m)
                    decay = jnp.exp2(past - m)
                    part = before[1][place_of(work)] * decay
                    mixed = before[2][place_of(work)] * decay
                current = (work, m, part, mixed)

    if final:
        out_shape = (jax.ShapeDtypeStruct((n_heads, tokens, group, head_dim), bf16),) * 2
    else:
        out_shape = (jax.ShapeDtypeStruct((n_heads, 2 * q_rows, 128), f32),) * 3
    alias = {1 + n_plain + j: j for j in range(3)} if state is not None and not final else {}
    pairs = 2 * half * q_rows * (sum(lengths) + extra * len(plan))
    slot = pltpu.VMEM((q_rows, max(lengths) + extra), f32)
    return pl.pallas_call(
        kernel,
        out_shape=out_shape,
        in_specs=[whole(pltpu.SMEM)] + [whole() for _ in operands],
        out_specs=(whole(),) * len(out_shape),
        scratch_shapes=[pltpu.VMEM((half, 2 * head_dim, n), bf16) for n in lengths]
        + [pltpu.VMEM((half, n, head_dim), bf16) for n in lengths]
        + [pltpu.VMEM((half, head_dim, codes), f32), slot, slot],
        input_output_aliases=alias,
        compiler_params=params(megabytes),
        cost_estimate=pl.CostEstimate(flops=8 * pairs * head_dim, bytes_accessed=4 * 2**20, transcendentals=pairs),
        name="attend",
    )(place, *operands)


def lay_out(place, heads_of, foreign, out):
    n_out, tokens, group, head_dim = heads_of.shape
    half = n_out // 2

    def kernel(place, source, *refs):
        target, sems = refs[-2:]
        core, inner = place[0], place[1]
        which = 1 - core if foreign else core
        copies = []
        for j in range(n_out):
            head = (inner if j < half else 1 - inner) * n_out + which * half + j % half
            copies.append(pltpu.make_async_copy(source.at[j], target.at[:, head], sems.at[j]))
            copies[-1].start()
        for copy in copies:
            copy.wait()

    return pl.pallas_call(
        kernel,
        out_shape=jax.ShapeDtypeStruct((tokens, 2 * n_out, group, head_dim), bf16),
        in_specs=[whole(pltpu.SMEM), whole()] + ([] if out is None else [whole(pl.ANY)]),
        out_specs=whole(pl.ANY),
        scratch_shapes=[pltpu.SemaphoreType.DMA((n_out,))],
        input_output_aliases={} if out is None else {2: 0},
        compiler_params=params(),
        name="lay_out",
    )(place, heads_of, *([] if out is None else [out]))


def paired(qkv, key_codes, codebooks, value_codes, value_scales, block_ids, *, n_outer):
    tokens, n_heads, slots, head_dim = qkv.shape
    group = slots - 2
    rows, kv_local, groups = key_codes.shape
    codes = codebooks.shape[1]
    half = kv_local // 2
    n_far = n_outer // 4
    prefix = rows * n_outer
    outer, inner = lax.axis_index("outer"), lax.axis_index("inner")
    core = outer % 2
    place = jnp.stack([core, inner]).astype(jnp.int32)
    extent = half * (rows + groups)

    def swap(x, outer_bits, inner_bits=0):
        return lax.ppermute(
            x,
            axes,
            [
                (2 * o + i, 2 * (o ^ outer_bits) + (i ^ inner_bits))
                for o in range(n_outer)
                for i in range(2)
            ],
        )

    keep, send = prepare(place, block_ids, key_codes, value_codes, value_scales, qkv, prefix, half)
    mate = swap(send, 1)
    queries = (keep, mate)

    pack = jnp.concatenate([keep[:extent], mate[:extent], keep[extent : extent + 8], mate[extent : extent + 8]], axis=0)
    size = pack.shape[0]

    def blocks_of(base, count=1):
        out = []
        for j in range(count):
            b = base + j * size
            out.append((b, b + half * rows, b + 2 * extent))
            out.append((b + extent, b + extent + half * rows, b + 2 * extent + 8))
        return out

    def along(parts, bits):
        return swap(jnp.concatenate(parts, axis=0) if len(parts) > 1 else parts[0], 4 * bits)

    my_books = lax.dynamic_slice_in_dim(codebooks, core * half, half, 0).reshape(half * codes, head_dim)
    z_far = [along([pack], n_far // 2)]
    diag = swap(pack, 2, 1)
    x_pack = swap(pack, 2)
    y_pack = swap(jnp.concatenate([pack, my_books], axis=0), 0, 1)
    z_far[0], diag = lax.optimization_barrier((z_far[0], diag))
    diag_far = [along([diag], n_far // 2)]
    bits = n_far // 4
    while bits:
        z_far.append(along([pack] + z_far, bits))
        bits //= 2

    x_first, y_first = swap(z_far[0], 2), swap(z_far[0], 0, 1)
    positions = np.arange(rows)
    cos_tok, sin_tok = np.cos(angle_table(positions, head_dim)), np.sin(angle_table(positions, head_dim))
    starts = np.arange(128) * rows
    cos_blk, sin_blk = np.cos(angle_table(starts, head_dim)), np.sin(angle_table(starts, head_dim))
    tables = [jnp.asarray(t.astype(np.float32)) for t in (cos_tok, sin_tok, cos_blk, sin_blk)]
    sizes = (half, rows, groups, tokens, group, head_dim, codes)
    call = functools.partial(attend, place, tables=tables, queries=queries, sizes=sizes)
    own_book = (codebooks, None)

    def pieces(*arrays):
        return [(a, blocks_of(0, a.shape[0] // size)) for a in arrays]

    own_kv = 2 * half * 2 * tokens
    kv_own = jnp.concatenate([keep[-own_kv:], mate[-own_kv:]], axis=0)
    kv_own, y_pack = lax.optimization_barrier((kv_own, y_pack))
    kv_pair = swap(kv_own, 0, 1)
    state = call([(0, own_book, pieces(pack, x_pack, z_far[0], x_first), False)], stretch=None, state=None, final=False)
    other_book, y_near = (y_pack, size), [(y_pack, blocks_of(0))]
    *z_rest, y_first = lax.optimization_barrier((*z_far[1:], y_first))
    z_rest = jnp.concatenate(z_rest, axis=0) if len(z_rest) > 1 else z_rest[0]
    y_rest = swap(z_rest, 0, 1)
    x_rest = swap(z_rest, 2)
    diag_far[0], kv_pair, *state = lax.optimization_barrier((diag_far[0], kv_pair, *state))
    bits = n_far // 4
    while bits:
        diag_far.append(along([diag] + diag_far, bits))
        bits //= 2
    state = call(
        [
            (0, own_book, pieces(*z_far[1:]), True),
            (half, other_book, y_near + pieces(diag, diag_far[0], y_first), False),
        ],
        stretch=kv_pair, state=state, final=False,
    )
    out, out_send = call(
        [(0, own_book, pieces(x_rest), True), (half, other_book, pieces(*diag_far[1:], y_rest), True)],
        stretch=None, state=state, final=True,
    )
    out_mate = swap(out_send, 1)
    return lay_out(place, out_mate, True, lay_out(place, out, False, None))


def rotate(tensor, position):
    half_dim = tensor.shape[-1] // 2
    ladder = jnp.arange(half_dim, dtype=jnp.float32)
    inverse = jnp.exp(ladder * jnp.float32(-2.0 * math.log(rope_base) / tensor.shape[-1]))
    angles = position.astype(jnp.float32)[:, None] * inverse[None, :]
    target = (position.shape[0],) + (1,) * (tensor.ndim - 2) + (half_dim,)
    cosine = jnp.cos(angles).reshape(target)
    sine_part = jnp.sin(angles).reshape(target)
    floats = tensor.astype(jnp.float32)
    first_half = floats[..., :half_dim]
    second_half = floats[..., half_dim:]
    return jnp.concatenate(
        [
            first_half * cosine - second_half * sine_part,
            second_half * cosine + first_half * sine_part,
        ],
        axis=-1,
    )


def decode_block(key_codes, codebooks):
    block_rows, kv_local, group_count = key_codes.shape
    entries = codebooks.shape[1]
    head_dim = codebooks.shape[2]
    ladder = lax.broadcasted_iota(jnp.int32, (1, 1, 1, entries), 3).astype(jnp.float32)
    one_hot = (key_codes.astype(jnp.float32)[..., None] == ladder).astype(jnp.bfloat16)
    code_table = codebooks.reshape(kv_local, entries, group_count, head_dim // group_count)
    decoded = jnp.einsum("bkgc,kcgd->bkgd", one_hot, code_table, preferred_element_type=jnp.float32)
    return decoded.reshape(block_rows, kv_local, head_dim)


def span_of():
    return 1024


def absorb(state, queries, key_rows, value_rows, allowed):
    running_max, running_sum, weighted = state
    scores = jnp.einsum(
        "tkgd,nkd->tkgn", queries, key_rows, preferred_element_type=jnp.float32
    ) * queries.shape[-1] ** (-0.5)
    if allowed is not None:
        scores = jnp.where(allowed[:, None, None, :], scores, -jnp.inf)
    new_max = jnp.maximum(running_max, jnp.max(scores, axis=-1))
    decay_factor = jnp.exp(running_max - new_max)
    weights = jnp.exp(scores - new_max[..., None])
    running_sum = running_sum * decay_factor + jnp.sum(weights, axis=-1)
    weighted = weighted * decay_factor[..., None] + jnp.einsum(
        "tkgn,nkd->tkgd",
        weights.astype(jnp.bfloat16),
        value_rows,
        preferred_element_type=jnp.float32,
    )
    return (new_max, running_sum, weighted)


def shards(qkv, key_codes, codebooks, value_codes, value_scales, block_ids):
    group_heads = qkv.shape[2] - 2
    head_dim = qkv.shape[3]
    block_rows = key_codes.shape[0]
    prefix_len = block_rows * lax.axis_size("outer")
    prefix_values = (value_codes.astype(jnp.float32) * value_scales[:, :, None]).astype(
        jnp.bfloat16
    )
    exchanged = lax.all_to_all(qkv, "inner", split_axis=1, concat_axis=0, tiled=True)
    stretch_rows = exchanged.shape[0]
    kv_local = exchanged.shape[1]
    local_pos = jnp.arange(stretch_rows, dtype=jnp.int32)
    stretch_pos = prefix_len + local_pos
    queries = rotate(exchanged[:, :, :group_heads, :], stretch_pos).astype(jnp.bfloat16)
    stretch_keys = rotate(exchanged[:, :, group_heads, :], stretch_pos).astype(jnp.bfloat16)
    stretch_values = exchanged[:, :, group_heads + 1, :]
    initial = (
        jnp.full((stretch_rows, kv_local, group_heads), -1e30, jnp.float32),
        jnp.zeros((stretch_rows, kv_local, group_heads), jnp.float32),
        jnp.zeros((stretch_rows, kv_local, group_heads, head_dim), jnp.float32),
    )
    own_pos = block_ids[0] * block_rows + jnp.arange(block_rows, dtype=jnp.int32)
    prefix_keys = rotate(decode_block(key_codes, codebooks), own_pos).astype(jnp.bfloat16)
    key_rows = lax.all_gather(prefix_keys, "outer", axis=0, tiled=True)
    value_rows = lax.all_gather(prefix_values, "outer", axis=0, tiled=True)
    length = key_rows.shape[0]
    span_rows = span_of()

    def advance(step_index, inner_state):
        first_row = step_index * span_rows
        key_part = lax.dynamic_slice_in_dim(key_rows, first_row, span_rows, 0)
        value_part = lax.dynamic_slice_in_dim(value_rows, first_row, span_rows, 0)
        return absorb(inner_state, queries, key_part, value_part, None)

    allowed = local_pos[None, :] <= local_pos[:, None]
    final_state = lax.fori_loop(
        0,
        length // span_rows,
        advance,
        absorb(initial, queries, stretch_keys, stretch_values, allowed),
    )
    running_max, running_sum, weighted = final_state
    outputs = (weighted / running_sum[..., None]).astype(jnp.bfloat16)
    return lax.all_to_all(outputs, "inner", split_axis=0, concat_axis=1, tiled=True)


def solution(mesh):
    n_outer, n_inner = mesh.shape["outer"], mesh.shape["inner"]

    def body(qkv, key_codes, codebooks, value_codes, value_scales, block_ids):
        arrays = (qkv, key_codes, codebooks, value_codes, value_scales, block_ids)
        head_dim = qkv.shape[3]
        far = n_outer // 4
        fits = (
            n_inner == 2
            and n_outer % 4 == 0
            and 4 <= far
            and far & (far - 1) == 0
            and n_outer <= 128
            and key_codes.shape[1] % 2 == 0
            and key_codes.shape[0] == 128
            and head_dim == 128
            and head_dim // key_codes.shape[2] == 8
            and key_codes.shape[2] % 16 == 0
            and codebooks.shape[1] % 128 == 0
            and qkv.shape[2] == 10
            and qkv.shape[0] % 32 == 0
        )
        if fits:
            return paired(*arrays, n_outer=n_outer)
        return shards(*arrays)

    return jax.shard_map(
        body,
        mesh=mesh,
        in_specs=(
            P(("outer", "inner"), None, None, None),
            P("outer", "inner", None),
            P("inner", None, None),
            P("outer", "inner", None),
            P("outer", "inner"),
            P("outer"),
        ),
        out_specs=P(("outer", "inner"), None, None, None),
        check_vma=False,
    )
```

```python
import functools
import math

import jax
import jax.numpy as jnp
import numpy as np
from jax import lax
from jax.experimental import pallas as pl
from jax.experimental.pallas import tpu as pltpu
from jax.sharding import PartitionSpec as P

rope_base = 500000.0
axes = ("outer", "inner")
bf16 = jnp.bfloat16
f32 = jnp.float32


def frequencies(head_dim):
    ladder = np.arange(head_dim // 2, dtype=np.float32)
    return np.exp(ladder * np.float32(-2.0 * math.log(rope_base) / head_dim)).astype(np.float32)


def angle_table(positions, head_dim):
    return frequencies(head_dim)[:, None] * positions.astype(np.float32)[None, :]


def whole(memory=pltpu.VMEM):
    return pl.BlockSpec(memory_space=memory)


def params(megabytes=16):
    return pltpu.CompilerParams(vmem_limit_bytes=megabytes * 2**20)


def prepare(place, ids, codes, values, scales, qkv, prefix, half):
    rows, kv_local, groups = codes.shape
    tokens, n_heads, slots, head_dim = qkv.shape
    group = slots - 2
    q_rows = tokens * group
    extent = half * (rows + groups)
    n_out = 2 * half
    kv_at = extent + 16 + n_out * q_rows
    size = kv_at + n_out * 2 * tokens
    angles = angle_table(np.arange(2 * tokens) + prefix, head_dim)
    cosine, sine = np.cos(angles).T, np.sin(angles).T
    cosine = jnp.asarray(np.concatenate([cosine, cosine], axis=1).astype(np.float32))
    sine = jnp.asarray(np.concatenate([-sine, sine], axis=1).astype(np.float32))
    sources = (codes.transpose(1, 2, 0), values, scales.T, qkv.transpose(0, 2, 1, 3), cosine, sine)

    def kernel(place, ids, *refs):
        given, (keep, send), held = refs[:6], refs[6:8], refs[8:14]
        codes, values, scales, qkv, cosine, sine = held
        q_scratch, k_scratch, v_scratch, sems = refs[14:]
        core, inner = place[0], place[1]
        copies = [pltpu.make_async_copy(*pair, sems.at[i]) for i, pair in enumerate(zip(given, held))]
        for copy in copies:
            copy.start()
        for copy in copies[:3]:
            copy.wait()
        diagonal = lax.broadcasted_iota(jnp.int32, (rows, rows), 0) == lax.broadcasted_iota(jnp.int32, (rows, rows), 1)

        def put(target, head, k):
            factor = jnp.broadcast_to(scales[head : head + 1, :], (rows, rows))
            factor = jnp.sum(jnp.where(diagonal, factor, 0.0), axis=1, keepdims=True)
            target[k * rows : (k + 1) * rows, :] = (values[:, head, :].astype(f32) * factor).astype(bf16)
            first = half * rows + k * groups
            target[first : first + groups, :] = codes[head].astype(f32).astype(bf16)

        for side in range(2):

            @pl.when(core == side)
            def _():
                for k in range(half):
                    put(send, (1 - side) * half + k, k)
                    put(keep, side * half + k, k)

        number = jnp.full((16, head_dim), ids[0], jnp.int32).astype(f32).astype(bf16)
        send[extent : extent + 16, :] = number
        keep[extent : extent + 16, :] = number
        for copy in copies[3:]:
            copy.wait()
        at = pl.ds(pl.multiple_of(inner * tokens, tokens), tokens)
        cos, sin = cosine[at, :][:, None, :], sine[at, :][:, None, :]

        def turn(x):
            return x * cos + pltpu.roll(x, head_dim // 2, 2) * sin

        spread = (tokens, 1, n_heads, head_dim)
        for slot in range(group):
            x = turn(qkv[:, slot, :, :].astype(f32))
            q_scratch[:, slot : slot + 1, :, :] = x.reshape(spread)
        k_scratch[...] = turn(qkv[:, group, :, :].astype(f32))
        v_scratch[...] = qkv[:, group + 1, :, :].astype(f32)
        q_flat = q_scratch.reshape(q_rows * n_heads, head_dim)
        k_flat = k_scratch.reshape(tokens * n_heads, head_dim)
        v_flat = v_scratch.reshape(tokens * n_heads, head_dim)
        for target, which in ((send, 1 - core), (keep, core)):
            for j in range(n_out):
                head = (inner if j < half else 1 - inner) * kv_local + which * half + j % half
                first = extent + 16 + j * q_rows
                target[first : first + q_rows, :] = q_flat[pl.ds(head, q_rows, stride=n_heads), :].astype(bf16)
                first = kv_at + j * 2 * tokens
                target[first : first + tokens, :] = k_flat[pl.ds(head, tokens, stride=n_heads), :].astype(bf16)
                first += tokens
                target[first : first + tokens, :] = v_flat[pl.ds(head, tokens, stride=n_heads), :].astype(bf16)

    shape = jax.ShapeDtypeStruct((size, head_dim), bf16)
    return pl.pallas_call(
        kernel,
        out_shape=(shape, shape),
        in_specs=[whole(pltpu.SMEM)] * 2 + [whole(pltpu.HBM)] * 6,
        out_specs=(whole(), whole()),
        scratch_shapes=[pltpu.VMEM(x.shape, x.dtype) for x in sources]
        + [
            pltpu.VMEM((tokens, group, n_heads, head_dim), f32),
            pltpu.VMEM((tokens, n_heads, head_dim), f32),
            pltpu.VMEM((tokens, n_heads, head_dim), f32),
            pltpu.SemaphoreType.DMA((6,)),
        ],
        compiler_params=params(),
        name="prepare",
    )(place, ids, *[pltpu.with_memory_space_constraint(x, pltpu.HBM) for x in sources])


def attend(place, groups_of, tables, queries, stretch, state, sizes, final, megabytes=32):
    half, rows, groups, tokens, group, head_dim, codes = sizes
    q_rows = tokens * group
    scale = head_dim**-0.5 * math.log2(math.e)
    gd = head_dim // groups
    half_dim = head_dim // 2
    n_heads = 2 * half
    q_at = half * (rows + groups) + 16
    kv_at = q_at + n_heads * q_rows
    lengths = [sum(len(blocks) for _, blocks in pieces) * rows for _, _, pieces, _ in groups_of]
    extra = 2 * tokens if stretch is not None else 0
    chunk = 512

    operands, where = [], {}

    def ref_of(array):
        if id(array) not in where:
            where[id(array)] = len(operands)
            operands.append(array)
        return where[id(array)]

    plan = [
        (first, ref_of(book), row, [(ref_of(array), blocks) for array, blocks in pieces])
        for first, (book, row), pieces, _ in groups_of
    ]
    table_at = [ref_of(t) for t in tables]
    query_at = [ref_of(q) for q in queries]
    stretch_at = ref_of(stretch[0]) if stretch is not None else None
    n_plain = len(operands)
    if state is not None:
        operands += list(state)

    def kernel(place, *refs):
        refs = list(refs)
        given = refs[:n_plain]
        before = refs[n_plain : n_plain + 3] if state is not None else None
        refs = refs[len(operands) :]
        results = refs[: 2 if final else 3]
        refs = refs[len(results) :]
        kts, vvs = refs[: len(plan)], refs[len(plan) : 2 * len(plan)]
        tab, slots = refs[2 * len(plan)], refs[2 * len(plan) + 1 :]
        core, inner = place[0], place[1]
        cos_tok, sin_tok, cos_blk, sin_blk = [given[i] for i in table_at]
        requests = [given[i] for i in query_at]
        other = given[stretch_at] if stretch is not None else None

        def load_books(group_index):
            first, book_at, book_row, pieces = plan[group_index]
            book = given[book_at]
            for k in range(half):
                if book_row is None:
                    entries = book[core * half + k]
                else:
                    entries = book[book_row + k * codes : book_row + (k + 1) * codes, :]
                tab[group_index * half + k] = entries.astype(f32).T

        def decode(group_index, index, at, value_row, code_row, id_row):
            kt, vv, ref = kts[group_index], vvs[group_index], given[at]
            base = id_row - id_row % 16
            block = ref[base : base + 16, :].astype(f32)
            block = block[id_row % 16 : id_row % 16 + 8].astype(jnp.int32)
            block = jnp.broadcast_to(block[None], (half_dim // 8, 8, head_dim)).reshape(half_dim, head_dim)
            cb = jnp.take_along_axis(cos_blk[...], block, axis=1, mode="promise_in_bounds")
            sb = jnp.take_along_axis(sin_blk[...], block, axis=1, mode="promise_in_bounds")
            ct, st = cos_tok[...], sin_tok[...]
            cos = cb * ct - sb * st
            sin = sb * ct + cb * st
            span = slice(index * rows, (index + 1) * rows)
            for k in range(half):
                table = group_index * half + k
                code = ref[code_row + k * groups : code_row + (k + 1) * groups, :].astype(f32).astype(jnp.int32)
                code = jnp.broadcast_to(code[:, None, :], (groups, gd, rows)).reshape(head_dim, rows)
                low = code & 127
                key = jnp.take_along_axis(tab[table, :, :128], low, axis=1, mode="promise_in_bounds")
                for part in range(1, codes // 128):
                    entries = tab[table, :, part * 128 : (part + 1) * 128]
                    more = jnp.take_along_axis(entries, low, axis=1, mode="promise_in_bounds")
                    key = jnp.where(code >= part * 128, more, key)
                a, b = key[:half_dim], key[half_dim:]
                key = jnp.concatenate([a * cos - b * sin, b * cos + a * sin], axis=0).astype(bf16)
                kt[k, :head_dim, span] = key
                kt[k, head_dim:, span] = key
                vv[k, span, :] = ref[value_row + k * rows : value_row + (k + 1) * rows, :]

        def blocks_in(group_index):
            every = [(at, *block) for at, blocks in plan[group_index][3] for block in blocks]
            return [functools.partial(decode, group_index, i, *block) for i, block in enumerate(every)]

        for group_index in range(len(plan)):
            load_books(group_index)
        for task in blocks_in(0):
            task()
        later = blocks_in(1) if len(plan) > 1 else []

        works = [(g, k) for g in range(len(plan)) for k in range(half)]

        def parts(work):
            return [(c, min(chunk, lengths[work[0]] - c)) for c in range(0, lengths[work[0]], chunk)]

        def scaled_queries(work):
            g, k = work
            first = q_at + (plan[g][0] + k) * q_rows
            scaled = jnp.concatenate([ref[first : first + q_rows, :] for ref in requests], axis=0).astype(f32) * scale
            hi = scaled.astype(bf16)
            lo = (scaled - hi.astype(f32)).astype(bf16)
            return jnp.concatenate([hi, lo], axis=1)

        def fold(top, score):
            for i in range(score.shape[1] // 128):
                piece = score[:, i * 128 : (i + 1) * 128]
                top = piece if top is None else jnp.maximum(top, piece)
            return top

        def score_part(work, q, slot, top, c, width):
            score = jnp.dot(q, kts[work[0]][work[1], :, c : c + width], preferred_element_type=f32)
            slot[:, c : c + width] = score
            return fold(top, score)

        def stretch_rows(work, e, which):
            g, k = work
            head = plan[g][0] + k
            base = stretch[1] + (e * n_heads + (head + half) % n_heads) * 2 * tokens + which * tokens
            mine = kv_at + head * 2 * tokens + which * tokens
            return jnp.concatenate([other[base : base + tokens, :], requests[e][mine : mine + tokens, :]], axis=0)

        def score_stretch(work, q, slot, top):
            for e in range(2):
                key = stretch_rows(work, e, 0)
                key = jnp.concatenate([key, key], axis=1)
                score = lax.dot_general(
                    q[e * q_rows : (e + 1) * q_rows], key, (((1,), (1,)), ((), ())), preferred_element_type=f32
                )
                column = lax.broadcasted_iota(jnp.int32, score.shape, 1)
                row = lax.broadcasted_iota(jnp.int32, score.shape, 0) // group
                allowed = (column - tokens <= row) & (column >= tokens * (1 - inner))
                tops.append(jnp.where(allowed, score, -jnp.inf))
                slot[e * q_rows : (e + 1) * q_rows, lengths[work[0]] : lengths[work[0]] + extra] = tops[-1]
            return fold(top, jnp.concatenate(tops[-2:], axis=0))

        tops = []

        def weigh(slot, m, part, mixed, c, width, value):
            weights = []
            for i in range(c, c + width, 128):
                weight = jnp.exp2(slot[:, i : i + 128] - m)
                part = part + weight
                weights.append(weight.astype(bf16))
            weight = jnp.concatenate(weights, axis=1) if len(weights) > 1 else weights[0]
            if isinstance(value, list):
                new = [jnp.dot(weight[i * q_rows : (i + 1) * q_rows], v, preferred_element_type=f32) for i, v in enumerate(value)]
                return part, mixed + jnp.concatenate(new, axis=0)
            return part, mixed + jnp.dot(weight, value, preferred_element_type=f32)

        def place_of(work):
            g, k = work
            return plan[g][0] + k

        current = None
        for t in range(len(works) + 1):
            slot, old = slots[t % 2], slots[1 - t % 2]
            work = works[t] if t < len(works) else None
            top = None
            if work is not None:
                q = scaled_queries(work)
            if current is not None:
                done, m, part, mixed = current
            if stretch is not None:
                if work is not None:
                    top = score_stretch(work, q, slot, top)
                if current is not None:
                    part, mixed = weigh(old, m, part, mixed, lengths[done[0]], extra, [stretch_rows(done, e, 1) for e in range(2)])
            ahead = parts(work) if work is not None else []
            behind = parts(done) if current is not None else []
            first_steps = half * len(parts(works[0]))
            for i in range(max(len(ahead), len(behind))):
                for _ in range(-(-len(blocks_in(1)) // first_steps) if later else 0):
                    if later:
                        later.pop(0)()
                if i < len(ahead):
                    top = score_part(work, q, slot, top, *ahead[i])
                if i < len(behind):
                    c, width = behind[i]
                    part, mixed = weigh(old, m, part, mixed, c, width, vvs[done[0]][done[1], c : c + width, :])
            if current is not None:
                if final:
                    head = plan[done[0]][0] + done[1]
                    result = mixed / jnp.sum(part, axis=1, keepdims=True)
                    for e in range(2):
                        result_e = result[e * q_rows : (e + 1) * q_rows].reshape(tokens, group, head_dim)
                        results[e][head] = result_e.astype(bf16)
                else:
                    for ref, value in zip(results, (m, part, mixed)):
                        ref[place_of(done)] = value
            if work is not None:
                m = jnp.broadcast_to(jnp.max(top, axis=1, keepdims=True), (2 * q_rows, 128))
                if not groups_of[work[0]][3]:
                    part = jnp.zeros((2 * q_rows, 128), f32)
                    mixed = jnp.zeros((2 * q_rows, head_dim), f32)
                else:
                    past = before[0][place_of(work)]
                    m = jnp.maximum(past, m)
                    decay = jnp.exp2(past - m)
                    part = before[1][place_of(work)] * decay
                    mixed = before[2][place_of(work)] * decay
                current = (work, m, part, mixed)

    if final:
        out_shape = (jax.ShapeDtypeStruct((n_heads, tokens, group, head_dim), bf16),) * 2
    else:
        out_shape = (jax.ShapeDtypeStruct((n_heads, 2 * q_rows, 128), f32),) * 3
    alias = {1 + n_plain + j: j for j in range(3)} if state is not None and not final else {}
    pairs = 2 * half * q_rows * (sum(lengths) + extra * len(plan))
    slot = pltpu.VMEM((2 * q_rows, max(lengths) + extra), f32)
    return pl.pallas_call(
        kernel,
        out_shape=out_shape,
        in_specs=[whole(pltpu.SMEM)] + [whole() for _ in operands],
        out_specs=(whole(),) * len(out_shape),
        scratch_shapes=[pltpu.VMEM((half, 2 * head_dim, n), bf16) for n in lengths]
        + [pltpu.VMEM((half, n, head_dim), bf16) for n in lengths]
        + [pltpu.VMEM((len(lengths) * half, head_dim, codes), f32), slot, slot],
        input_output_aliases=alias,
        compiler_params=params(megabytes),
        cost_estimate=pl.CostEstimate(flops=8 * pairs * head_dim, bytes_accessed=4 * 2**20, transcendentals=pairs),
        name="attend",
    )(place, *operands)


def lay_out(place, heads_of, foreign, out):
    n_out, tokens, group, head_dim = heads_of.shape
    half = n_out // 2

    def kernel(place, source, *refs):
        target, sems = refs[-2:]
        core, inner = place[0], place[1]
        which = 1 - core if foreign else core
        copies = []
        for j in range(n_out):
            head = (inner if j < half else 1 - inner) * n_out + which * half + j % half
            copies.append(pltpu.make_async_copy(source.at[j], target.at[:, head], sems.at[j]))
            copies[-1].start()
        for copy in copies:
            copy.wait()

    return pl.pallas_call(
        kernel,
        out_shape=jax.ShapeDtypeStruct((tokens, 2 * n_out, group, head_dim), bf16),
        in_specs=[whole(pltpu.SMEM), whole()] + ([] if out is None else [whole(pl.ANY)]),
        out_specs=whole(pl.ANY),
        scratch_shapes=[pltpu.SemaphoreType.DMA((n_out,))],
        input_output_aliases={} if out is None else {2: 0},
        compiler_params=params(),
        name="lay_out",
    )(place, heads_of, *([] if out is None else [out]))


def paired(qkv, key_codes, codebooks, value_codes, value_scales, block_ids, *, n_outer):
    tokens, n_heads, slots, head_dim = qkv.shape
    group = slots - 2
    rows, kv_local, groups = key_codes.shape
    codes = codebooks.shape[1]
    half = kv_local // 2
    n_far = n_outer // 4
    prefix = rows * n_outer
    outer, inner = lax.axis_index("outer"), lax.axis_index("inner")
    core = outer % 2
    place = jnp.stack([core, inner]).astype(jnp.int32)
    extent = half * (rows + groups)

    def swap(x, outer_bits, inner_bits=0):
        return lax.ppermute(
            x,
            axes,
            [
                (2 * o + i, 2 * (o ^ outer_bits) + (i ^ inner_bits))
                for o in range(n_outer)
                for i in range(2)
            ],
        )

    keep, send = prepare(place, block_ids, key_codes, value_codes, value_scales, qkv, prefix, half)
    mate = swap(send, 1)
    queries = (keep, mate)

    pack = jnp.concatenate([keep[:extent], mate[:extent], keep[extent : extent + 8], mate[extent : extent + 8]], axis=0)
    size = pack.shape[0]

    def blocks_of(base, count=1):
        out = []
        for j in range(count):
            b = base + j * size
            out.append((b, b + half * rows, b + 2 * extent))
            out.append((b + extent, b + extent + half * rows, b + 2 * extent + 8))
        return out

    my_books = lax.dynamic_slice_in_dim(codebooks, core * half, half, 0).reshape(half * codes, head_dim)
    own_kv = 2 * half * 2 * tokens
    stretch = jnp.concatenate([keep[-own_kv:], mate[-own_kv:]], axis=0)

    def along(parts, bits):
        return swap(jnp.concatenate(parts, axis=0) if len(parts) > 1 else parts[0], 4 * bits)

    steps = [n_far >> (i + 1) for i in range(n_far.bit_length() - 1)]
    z_one = [along([pack], bits) for bits in steps]
    x_pack = swap(pack, 2)
    y_pack = swap(jnp.concatenate([pack, my_books, stretch], axis=0), 0, 1)
    diag = swap(pack, 2, 1)

    positions = np.arange(rows)
    cos_tok, sin_tok = np.cos(angle_table(positions, head_dim)), np.sin(angle_table(positions, head_dim))
    starts = np.arange(128) * rows
    cos_blk, sin_blk = np.cos(angle_table(starts, head_dim)), np.sin(angle_table(starts, head_dim))
    tables = [jnp.asarray(t.astype(np.float32)) for t in (cos_tok, sin_tok, cos_blk, sin_blk)]
    sizes = (half, rows, groups, tokens, group, head_dim, codes)
    call = functools.partial(attend, place, tables=tables, queries=queries, sizes=sizes)
    own_book = (codebooks, None)

    def pieces(*arrays):
        return [(a, blocks_of(0, a.shape[0] // size)) for a in arrays]

    other_book, other_stretch = (y_pack, size), (y_pack, size + half * codes)

    state = call([(0, own_book, pieces(pack, x_pack, z_one[-1]), False)], stretch=None, state=None, final=False)
    *z_one, diag, first, second, third = lax.optimization_barrier((*z_one, diag, *state))
    state = (first, second, third)
    z_two, reached = [], [z_one[0]]
    for i, bits in enumerate(steps[1:]):
        z_two.append(along(reached, bits))
        reached = reached + [z_one[i + 1], z_two[-1]]
    diag_far = [along([diag], steps[0])]
    near = jnp.concatenate(z_one, axis=0)
    x_near, y_near = swap(near, 2), swap(near, 0, 1)
    state = call(
        [(0, own_book, pieces(*z_one[:-1]), True), (half, other_book, [(y_pack, blocks_of(0))] + pieces(diag), False)],
        stretch=other_stretch, state=state, final=False,
    )

    z_rest = jnp.concatenate(z_two, axis=0) if len(z_two) > 1 else z_two[0]
    x_rest, y_rest = swap(z_rest, 2), swap(z_rest, 0, 1)
    diag_far[0], first, second, third = lax.optimization_barrier((diag_far[0], *state))
    state = (first, second, third)
    for bits in steps[1:]:
        diag_far.append(along([diag] + diag_far, bits))
    state = call(
        [(0, own_book, pieces(z_rest, x_near), True), (half, other_book, pieces(diag_far[0], y_near), True)],
        stretch=None, state=state, final=False,
    )
    out, out_send = call(
        [(0, own_book, pieces(x_rest), True), (half, other_book, pieces(*diag_far[1:], y_rest), True)],
        stretch=None, state=state, final=True,
    )
    out_mate = swap(out_send, 1)
    return lay_out(place, out_mate, True, lay_out(place, out, False, None))


def rotate(tensor, position):
    half_dim = tensor.shape[-1] // 2
    ladder = jnp.arange(half_dim, dtype=jnp.float32)
    inverse = jnp.exp(ladder * jnp.float32(-2.0 * math.log(rope_base) / tensor.shape[-1]))
    angles = position.astype(jnp.float32)[:, None] * inverse[None, :]
    target = (position.shape[0],) + (1,) * (tensor.ndim - 2) + (half_dim,)
    cosine = jnp.cos(angles).reshape(target)
    sine_part = jnp.sin(angles).reshape(target)
    floats = tensor.astype(jnp.float32)
    first_half = floats[..., :half_dim]
    second_half = floats[..., half_dim:]
    return jnp.concatenate(
        [
            first_half * cosine - second_half * sine_part,
            second_half * cosine + first_half * sine_part,
        ],
        axis=-1,
    )


def decode_block(key_codes, codebooks):
    block_rows, kv_local, group_count = key_codes.shape
    entries = codebooks.shape[1]
    head_dim = codebooks.shape[2]
    ladder = lax.broadcasted_iota(jnp.int32, (1, 1, 1, entries), 3).astype(jnp.float32)
    one_hot = (key_codes.astype(jnp.float32)[..., None] == ladder).astype(jnp.bfloat16)
    code_table = codebooks.reshape(kv_local, entries, group_count, head_dim // group_count)
    decoded = jnp.einsum("bkgc,kcgd->bkgd", one_hot, code_table, preferred_element_type=jnp.float32)
    return decoded.reshape(block_rows, kv_local, head_dim)


def span_of():
    return 1024


def absorb(state, queries, key_rows, value_rows, allowed):
    running_max, running_sum, weighted = state
    scores = jnp.einsum(
        "tkgd,nkd->tkgn", queries, key_rows, preferred_element_type=jnp.float32
    ) * queries.shape[-1] ** (-0.5)
    if allowed is not None:
        scores = jnp.where(allowed[:, None, None, :], scores, -jnp.inf)
    new_max = jnp.maximum(running_max, jnp.max(scores, axis=-1))
    decay_factor = jnp.exp(running_max - new_max)
    weights = jnp.exp(scores - new_max[..., None])
    running_sum = running_sum * decay_factor + jnp.sum(weights, axis=-1)
    weighted = weighted * decay_factor[..., None] + jnp.einsum(
        "tkgn,nkd->tkgd",
        weights.astype(jnp.bfloat16),
        value_rows,
        preferred_element_type=jnp.float32,
    )
    return (new_max, running_sum, weighted)


def shards(qkv, key_codes, codebooks, value_codes, value_scales, block_ids):
    group_heads = qkv.shape[2] - 2
    head_dim = qkv.shape[3]
    block_rows = key_codes.shape[0]
    prefix_len = block_rows * lax.axis_size("outer")
    prefix_values = (value_codes.astype(jnp.float32) * value_scales[:, :, None]).astype(
        jnp.bfloat16
    )
    exchanged = lax.all_to_all(qkv, "inner", split_axis=1, concat_axis=0, tiled=True)
    stretch_rows = exchanged.shape[0]
    kv_local = exchanged.shape[1]
    local_pos = jnp.arange(stretch_rows, dtype=jnp.int32)
    stretch_pos = prefix_len + local_pos
    queries = rotate(exchanged[:, :, :group_heads, :], stretch_pos).astype(jnp.bfloat16)
    stretch_keys = rotate(exchanged[:, :, group_heads, :], stretch_pos).astype(jnp.bfloat16)
    stretch_values = exchanged[:, :, group_heads + 1, :]
    initial = (
        jnp.full((stretch_rows, kv_local, group_heads), -1e30, jnp.float32),
        jnp.zeros((stretch_rows, kv_local, group_heads), jnp.float32),
        jnp.zeros((stretch_rows, kv_local, group_heads, head_dim), jnp.float32),
    )
    own_pos = block_ids[0] * block_rows + jnp.arange(block_rows, dtype=jnp.int32)
    prefix_keys = rotate(decode_block(key_codes, codebooks), own_pos).astype(jnp.bfloat16)
    key_rows = lax.all_gather(prefix_keys, "outer", axis=0, tiled=True)
    value_rows = lax.all_gather(prefix_values, "outer", axis=0, tiled=True)
    length = key_rows.shape[0]
    span_rows = span_of()

    def advance(step_index, inner_state):
        first_row = step_index * span_rows
        key_part = lax.dynamic_slice_in_dim(key_rows, first_row, span_rows, 0)
        value_part = lax.dynamic_slice_in_dim(value_rows, first_row, span_rows, 0)
        return absorb(inner_state, queries, key_part, value_part, None)

    allowed = local_pos[None, :] <= local_pos[:, None]
    final_state = lax.fori_loop(
        0,
        length // span_rows,
        advance,
        absorb(initial, queries, stretch_keys, stretch_values, allowed),
    )
    running_max, running_sum, weighted = final_state
    outputs = (weighted / running_sum[..., None]).astype(jnp.bfloat16)
    return lax.all_to_all(outputs, "inner", split_axis=0, concat_axis=1, tiled=True)


def solution(mesh):
    n_outer, n_inner = mesh.shape["outer"], mesh.shape["inner"]

    def body(qkv, key_codes, codebooks, value_codes, value_scales, block_ids):
        arrays = (qkv, key_codes, codebooks, value_codes, value_scales, block_ids)
        head_dim = qkv.shape[3]
        far = n_outer // 4
        fits = (
            n_inner == 2
            and n_outer % 4 == 0
            and 4 <= far
            and far & (far - 1) == 0
            and n_outer <= 128
            and key_codes.shape[1] % 2 == 0
            and key_codes.shape[0] == 128
            and head_dim == 128
            and head_dim // key_codes.shape[2] == 8
            and key_codes.shape[2] % 16 == 0
            and codebooks.shape[1] % 128 == 0
            and qkv.shape[2] == 10
            and qkv.shape[0] % 32 == 0
        )
        if fits:
            return paired(*arrays, n_outer=n_outer)
        return shards(*arrays)

    return jax.shard_map(
        body,
        mesh=mesh,
        in_specs=(
            P(("outer", "inner"), None, None, None),
            P("outer", "inner", None),
            P("inner", None, None),
            P("outer", "inner", None),
            P("outer", "inner"),
            P("outer"),
        ),
        out_specs=P(("outer", "inner"), None, None, None),
        check_vma=False,
    )
```

```python
import functools
import math

import jax
import jax.numpy as jnp
import numpy as np
from jax import lax
from jax.experimental import pallas as pl
from jax.experimental.pallas import tpu as pltpu
from jax.sharding import PartitionSpec as P

rope_base = 500000.0
axes = ("outer", "inner")
bf16 = jnp.bfloat16
f32 = jnp.float32


def frequencies(head_dim):
    ladder = np.arange(head_dim // 2, dtype=np.float32)
    return np.exp(ladder * np.float32(-2.0 * math.log(rope_base) / head_dim)).astype(np.float32)


def angle_table(positions, head_dim):
    return frequencies(head_dim)[:, None] * positions.astype(np.float32)[None, :]


def whole(memory=pltpu.VMEM):
    return pl.BlockSpec(memory_space=memory)


def params(megabytes=16):
    return pltpu.CompilerParams(vmem_limit_bytes=megabytes * 2**20)


def prepare(place, ids, codes, values, scales, qkv, prefix, half):
    rows, kv_local, groups = codes.shape
    tokens, n_heads, slots, head_dim = qkv.shape
    group = slots - 2
    q_rows = tokens * group
    extent = half * (rows + groups)
    n_out = 2 * half
    kv_at = extent + 16 + n_out * q_rows
    size = kv_at + n_out * 2 * tokens
    angles = angle_table(np.arange(2 * tokens) + prefix, head_dim)
    cosine, sine = np.cos(angles).T, np.sin(angles).T
    cosine = jnp.asarray(np.concatenate([cosine, cosine], axis=1).astype(np.float32))
    sine = jnp.asarray(np.concatenate([-sine, sine], axis=1).astype(np.float32))
    sources = (codes.transpose(1, 2, 0), values, scales.T, qkv.transpose(0, 2, 1, 3), cosine, sine)

    def kernel(place, ids, *refs):
        given, (keep, send), held = refs[:6], refs[6:8], refs[8:14]
        codes, values, scales, qkv, cosine, sine = held
        q_scratch, k_scratch, v_scratch, sems = refs[14:]
        core, inner = place[0], place[1]
        copies = [pltpu.make_async_copy(*pair, sems.at[i]) for i, pair in enumerate(zip(given, held))]
        for copy in copies:
            copy.start()
        for copy in copies[:3]:
            copy.wait()
        diagonal = lax.broadcasted_iota(jnp.int32, (rows, rows), 0) == lax.broadcasted_iota(jnp.int32, (rows, rows), 1)

        def put(target, head, k):
            factor = jnp.broadcast_to(scales[head : head + 1, :], (rows, rows))
            factor = jnp.sum(jnp.where(diagonal, factor, 0.0), axis=1, keepdims=True)
            target[k * rows : (k + 1) * rows, :] = (values[:, head, :].astype(f32) * factor).astype(bf16)
            first = half * rows + k * groups
            target[first : first + groups, :] = codes[head].astype(f32).astype(bf16)

        for side in range(2):

            @pl.when(core == side)
            def _():
                for k in range(half):
                    put(send, (1 - side) * half + k, k)
                    put(keep, side * half + k, k)

        number = jnp.full((16, head_dim), ids[0], jnp.int32).astype(f32).astype(bf16)
        send[extent : extent + 16, :] = number
        keep[extent : extent + 16, :] = number
        for copy in copies[3:]:
            copy.wait()
        at = pl.ds(pl.multiple_of(inner * tokens, tokens), tokens)
        cos, sin = cosine[at, :][:, None, :], sine[at, :][:, None, :]

        def turn(x):
            return x * cos + pltpu.roll(x, head_dim // 2, 2) * sin

        spread = (tokens, 1, n_heads, head_dim)
        for slot in range(group):
            x = turn(qkv[:, slot, :, :].astype(f32))
            q_scratch[:, slot : slot + 1, :, :] = x.reshape(spread)
        k_scratch[...] = turn(qkv[:, group, :, :].astype(f32))
        v_scratch[...] = qkv[:, group + 1, :, :].astype(f32)
        q_flat = q_scratch.reshape(q_rows * n_heads, head_dim)
        k_flat = k_scratch.reshape(tokens * n_heads, head_dim)
        v_flat = v_scratch.reshape(tokens * n_heads, head_dim)
        for target, which in ((send, 1 - core), (keep, core)):
            for j in range(n_out):
                head = (inner if j < half else 1 - inner) * kv_local + which * half + j % half
                first = extent + 16 + j * q_rows
                target[first : first + q_rows, :] = q_flat[pl.ds(head, q_rows, stride=n_heads), :].astype(bf16)
                first = kv_at + j * 2 * tokens
                target[first : first + tokens, :] = k_flat[pl.ds(head, tokens, stride=n_heads), :].astype(bf16)
                first += tokens
                target[first : first + tokens, :] = v_flat[pl.ds(head, tokens, stride=n_heads), :].astype(bf16)

    shape = jax.ShapeDtypeStruct((size, head_dim), bf16)
    return pl.pallas_call(
        kernel,
        out_shape=(shape, shape),
        in_specs=[whole(pltpu.SMEM)] * 2 + [whole(pltpu.HBM)] * 6,
        out_specs=(whole(), whole()),
        scratch_shapes=[pltpu.VMEM(x.shape, x.dtype) for x in sources]
        + [
            pltpu.VMEM((tokens, group, n_heads, head_dim), f32),
            pltpu.VMEM((tokens, n_heads, head_dim), f32),
            pltpu.VMEM((tokens, n_heads, head_dim), f32),
            pltpu.SemaphoreType.DMA((6,)),
        ],
        compiler_params=params(),
        name="prepare",
    )(place, ids, *[pltpu.with_memory_space_constraint(x, pltpu.HBM) for x in sources])


def attend(place, groups_of, tables, queries, stretch, state, sizes, final, megabytes=32):
    half, rows, groups, tokens, group, head_dim, codes = sizes
    q_rows = tokens * group
    scale = head_dim**-0.5 * math.log2(math.e)
    gd = head_dim // groups
    half_dim = head_dim // 2
    n_heads = 2 * half
    q_at = half * (rows + groups) + 16
    kv_at = q_at + n_heads * q_rows
    lengths = [sum(len(blocks) for _, blocks in pieces) * rows for _, _, pieces, _ in groups_of]
    extra = 2 * tokens if stretch is not None else 0
    chunk = 256

    operands, where = [], {}

    def ref_of(array):
        if id(array) not in where:
            where[id(array)] = len(operands)
            operands.append(array)
        return where[id(array)]

    plan = [
        (first, ref_of(book), row, [(ref_of(array), blocks) for array, blocks in pieces])
        for first, (book, row), pieces, _ in groups_of
    ]
    table_at = [ref_of(t) for t in tables]
    query_at = [ref_of(q) for q in queries]
    stretch_at = ref_of(stretch[0]) if stretch is not None else None
    n_plain = len(operands)
    if state is not None:
        operands += list(state)

    def kernel(place, *refs):
        refs = list(refs)
        given = refs[:n_plain]
        before = refs[n_plain : n_plain + 3] if state is not None else None
        refs = refs[len(operands) :]
        results = refs[: 2 if final else 3]
        refs = refs[len(results) :]
        kts, vvs = refs[: len(plan)], refs[len(plan) : 2 * len(plan)]
        tab, slots = refs[2 * len(plan)], refs[2 * len(plan) + 1 :]
        core, inner = place[0], place[1]
        cos_tok, sin_tok, cos_blk, sin_blk = [given[i] for i in table_at]
        requests = [given[i] for i in query_at]
        other = given[stretch_at] if stretch is not None else None

        def load_books(group_index):
            first, book_at, book_row, pieces = plan[group_index]
            book = given[book_at]
            for k in range(half):
                if book_row is None:
                    entries = book[core * half + k]
                else:
                    entries = book[book_row + k * codes : book_row + (k + 1) * codes, :]
                tab[group_index * half + k] = entries.astype(f32).T

        def decode(group_index, index, at, value_row, code_row, id_row):
            kt, vv, ref = kts[group_index], vvs[group_index], given[at]
            base = id_row - id_row % 16
            block = ref[base : base + 16, :].astype(f32)
            block = block[id_row % 16 : id_row % 16 + 8].astype(jnp.int32)
            block = jnp.broadcast_to(block[None], (half_dim // 8, 8, head_dim)).reshape(half_dim, head_dim)
            cb = jnp.take_along_axis(cos_blk[...], block, axis=1, mode="promise_in_bounds")
            sb = jnp.take_along_axis(sin_blk[...], block, axis=1, mode="promise_in_bounds")
            ct, st = cos_tok[...], sin_tok[...]
            cos = cb * ct - sb * st
            sin = sb * ct + cb * st
            span = slice(index * rows, (index + 1) * rows)
            for k in range(half):
                table = group_index * half + k
                code = ref[code_row + k * groups : code_row + (k + 1) * groups, :].astype(f32).astype(jnp.int32)
                code = jnp.broadcast_to(code[:, None, :], (groups, gd, rows)).reshape(head_dim, rows)
                low = code & 127
                key = jnp.take_along_axis(tab[table, :, :128], low, axis=1, mode="promise_in_bounds")
                for part in range(1, codes // 128):
                    entries = tab[table, :, part * 128 : (part + 1) * 128]
                    more = jnp.take_along_axis(entries, low, axis=1, mode="promise_in_bounds")
                    key = jnp.where(code >= part * 128, more, key)
                a, b = key[:half_dim], key[half_dim:]
                key = jnp.concatenate([a * cos - b * sin, b * cos + a * sin], axis=0).astype(bf16)
                kt[k, :head_dim, span] = key
                kt[k, head_dim:, span] = key
                vv[k, span, :] = ref[value_row + k * rows : value_row + (k + 1) * rows, :]

        def blocks_in(group_index):
            every = [(at, *block) for at, blocks in plan[group_index][3] for block in blocks]
            return [functools.partial(decode, group_index, i, *block) for i, block in enumerate(every)]

        for group_index in range(len(plan)):
            load_books(group_index)
        for task in blocks_in(0):
            task()
        later = blocks_in(1) if len(plan) > 1 else []

        works = [(g, k) for g in range(len(plan)) for k in range(half)]

        def parts(work):
            return [(c, min(chunk, lengths[work[0]] - c)) for c in range(0, lengths[work[0]], chunk)]

        def scaled_queries(work):
            g, k = work
            first = q_at + (plan[g][0] + k) * q_rows
            scaled = jnp.concatenate([ref[first : first + q_rows, :] for ref in requests], axis=0).astype(f32) * scale
            hi = scaled.astype(bf16)
            lo = (scaled - hi.astype(f32)).astype(bf16)
            return jnp.concatenate([hi, lo], axis=1)

        def fold(top, score):
            for i in range(score.shape[1] // 128):
                piece = score[:, i * 128 : (i + 1) * 128]
                top = piece if top is None else jnp.maximum(top, piece)
            return top

        def score_part(work, q, slot, top, c, width):
            score = jnp.dot(q, kts[work[0]][work[1], :, c : c + width], preferred_element_type=f32)
            slot[:, c : c + width] = score
            return fold(top, score)

        def stretch_rows(work, e, which):
            g, k = work
            head = plan[g][0] + k
            base = stretch[1] + (e * n_heads + (head + half) % n_heads) * 2 * tokens + which * tokens
            mine = kv_at + head * 2 * tokens + which * tokens
            return jnp.concatenate([other[base : base + tokens, :], requests[e][mine : mine + tokens, :]], axis=0)

        def score_stretch(work, q, slot, top):
            for e in range(2):
                key = stretch_rows(work, e, 0)
                key = jnp.concatenate([key, key], axis=1)
                score = lax.dot_general(
                    q[e * q_rows : (e + 1) * q_rows], key, (((1,), (1,)), ((), ())), preferred_element_type=f32
                )
                column = lax.broadcasted_iota(jnp.int32, score.shape, 1)
                row = lax.broadcasted_iota(jnp.int32, score.shape, 0) // group
                allowed = (column - tokens <= row) & (column >= tokens * (1 - inner))
                tops.append(jnp.where(allowed, score, -jnp.inf))
                slot[e * q_rows : (e + 1) * q_rows, lengths[work[0]] : lengths[work[0]] + extra] = tops[-1]
            return fold(top, jnp.concatenate(tops[-2:], axis=0))

        tops = []

        def weigh(slot, m, part, mixed, c, width, value):
            weights = []
            for i in range(c, c + width, 128):
                weight = jnp.exp2(slot[:, i : i + 128] - m)
                part = part + weight
                weights.append(weight.astype(bf16))
            weight = jnp.concatenate(weights, axis=1) if len(weights) > 1 else weights[0]
            if isinstance(value, list):
                new = [jnp.dot(weight[i * q_rows : (i + 1) * q_rows], v, preferred_element_type=f32) for i, v in enumerate(value)]
                return part, mixed + jnp.concatenate(new, axis=0)
            return part, mixed + jnp.dot(weight, value, preferred_element_type=f32)

        def place_of(work):
            g, k = work
            return plan[g][0] + k

        current = None
        for t in range(len(works) + 1):
            slot, old = slots[t % 2], slots[1 - t % 2]
            work = works[t] if t < len(works) else None
            top = None
            if work is not None:
                q = scaled_queries(work)
            if current is not None:
                done, m, part, mixed = current
            if stretch is not None:
                if work is not None and work[0] in stretch[2]:
                    top = score_stretch(work, q, slot, top)
                if current is not None and done[0] in stretch[2]:
                    part, mixed = weigh(old, m, part, mixed, lengths[done[0]], extra, [stretch_rows(done, e, 1) for e in range(2)])
            ahead = parts(work) if work is not None else []
            behind = parts(done) if current is not None else []
            first_steps = half * len(parts(works[0]))
            for i in range(max(len(ahead), len(behind))):
                for _ in range(-(-len(blocks_in(1)) // first_steps) if later else 0):
                    if later:
                        later.pop(0)()
                if i < len(ahead):
                    top = score_part(work, q, slot, top, *ahead[i])
                if i < len(behind):
                    c, width = behind[i]
                    part, mixed = weigh(old, m, part, mixed, c, width, vvs[done[0]][done[1], c : c + width, :])
            if current is not None:
                if final:
                    head = plan[done[0]][0] + done[1]
                    result = mixed / jnp.sum(part, axis=1, keepdims=True)
                    for e in range(2):
                        result_e = result[e * q_rows : (e + 1) * q_rows].reshape(tokens, group, head_dim)
                        results[e][head] = result_e.astype(bf16)
                else:
                    for ref, value in zip(results, (m, part, mixed)):
                        ref[place_of(done)] = value
            if work is not None:
                m = jnp.broadcast_to(jnp.max(top, axis=1, keepdims=True), (2 * q_rows, 128))
                if not groups_of[work[0]][3]:
                    part = jnp.zeros((2 * q_rows, 128), f32)
                    mixed = jnp.zeros((2 * q_rows, head_dim), f32)
                else:
                    past = before[0][place_of(work)]
                    m = jnp.maximum(past, m)
                    decay = jnp.exp2(past - m)
                    part = before[1][place_of(work)] * decay
                    mixed = before[2][place_of(work)] * decay
                current = (work, m, part, mixed)

    if final:
        out_shape = (jax.ShapeDtypeStruct((n_heads, tokens, group, head_dim), bf16),) * 2
    else:
        out_shape = (jax.ShapeDtypeStruct((n_heads, 2 * q_rows, 128), f32),) * 3
    alias = {1 + n_plain + j: j for j in range(3)} if state is not None and not final else {}
    pairs = 2 * half * q_rows * (sum(lengths) + (extra * len(stretch[2]) if stretch is not None else 0))
    slot = pltpu.VMEM((2 * q_rows, max(lengths) + extra), f32)
    return pl.pallas_call(
        kernel,
        out_shape=out_shape,
        in_specs=[whole(pltpu.SMEM)] + [whole() for _ in operands],
        out_specs=(whole(),) * len(out_shape),
        scratch_shapes=[pltpu.VMEM((half, 2 * head_dim, n), bf16) for n in lengths]
        + [pltpu.VMEM((half, n, head_dim), bf16) for n in lengths]
        + [pltpu.VMEM((len(lengths) * half, head_dim, codes), f32), slot, slot],
        input_output_aliases=alias,
        compiler_params=params(megabytes),
        cost_estimate=pl.CostEstimate(flops=8 * pairs * head_dim, bytes_accessed=4 * 2**20, transcendentals=pairs),
        name="attend",
    )(place, *operands)


def lay_out(place, heads_of, foreign, out):
    n_out, tokens, group, head_dim = heads_of.shape
    half = n_out // 2

    def kernel(place, source, *refs):
        target, sems = refs[-2:]
        core, inner = place[0], place[1]
        which = 1 - core if foreign else core
        copies = []
        for j in range(n_out):
            head = (inner if j < half else 1 - inner) * n_out + which * half + j % half
            copies.append(pltpu.make_async_copy(source.at[j], target.at[:, head], sems.at[j]))
            copies[-1].start()
        for copy in copies:
            copy.wait()

    return pl.pallas_call(
        kernel,
        out_shape=jax.ShapeDtypeStruct((tokens, 2 * n_out, group, head_dim), bf16),
        in_specs=[whole(pltpu.SMEM), whole()] + ([] if out is None else [whole(pl.ANY)]),
        out_specs=whole(pl.ANY),
        scratch_shapes=[pltpu.SemaphoreType.DMA((n_out,))],
        input_output_aliases={} if out is None else {2: 0},
        compiler_params=params(),
        name="lay_out",
    )(place, heads_of, *([] if out is None else [out]))


def paired(qkv, key_codes, codebooks, value_codes, value_scales, block_ids, *, n_outer):
    tokens, n_heads, slots, head_dim = qkv.shape
    group = slots - 2
    rows, kv_local, groups = key_codes.shape
    codes = codebooks.shape[1]
    half = kv_local // 2
    n_far = n_outer // 4
    prefix = rows * n_outer
    outer, inner = lax.axis_index("outer"), lax.axis_index("inner")
    core = outer % 2
    place = jnp.stack([core, inner]).astype(jnp.int32)
    extent = half * (rows + groups)

    def swap(x, outer_bits, inner_bits=0):
        return lax.ppermute(
            x,
            axes,
            [
                (2 * o + i, 2 * (o ^ outer_bits) + (i ^ inner_bits))
                for o in range(n_outer)
                for i in range(2)
            ],
        )

    keep, send = prepare(place, block_ids, key_codes, value_codes, value_scales, qkv, prefix, half)
    mate = swap(send, 1)
    queries = (keep, mate)

    pack = jnp.concatenate([keep[:extent], mate[:extent], keep[extent : extent + 8], mate[extent : extent + 8]], axis=0)
    size = pack.shape[0]

    def blocks_of(base, count=1):
        out = []
        for j in range(count):
            b = base + j * size
            out.append((b, b + half * rows, b + 2 * extent))
            out.append((b + extent, b + extent + half * rows, b + 2 * extent + 8))
        return out

    my_books = lax.dynamic_slice_in_dim(codebooks, core * half, half, 0).reshape(half * codes, head_dim)
    own_kv = 2 * half * 2 * tokens
    stretch = jnp.concatenate([keep[-own_kv:], mate[-own_kv:]], axis=0)

    def along(parts, bits):
        return swap(jnp.concatenate(parts, axis=0) if len(parts) > 1 else parts[0], 4 * bits)

    steps = [n_far >> (i + 1) for i in range(n_far.bit_length() - 1)]
    z_one = [along([pack], bits) for bits in steps]
    x_pack = swap(pack, 2)
    y_pack = swap(jnp.concatenate([pack, my_books, stretch], axis=0), 0, 1)
    diag = swap(pack, 2, 1)

    positions = np.arange(rows)
    cos_tok, sin_tok = np.cos(angle_table(positions, head_dim)), np.sin(angle_table(positions, head_dim))
    starts = np.arange(128) * rows
    cos_blk, sin_blk = np.cos(angle_table(starts, head_dim)), np.sin(angle_table(starts, head_dim))
    tables = [jnp.asarray(t.astype(np.float32)) for t in (cos_tok, sin_tok, cos_blk, sin_blk)]
    sizes = (half, rows, groups, tokens, group, head_dim, codes)
    call = functools.partial(attend, place, tables=tables, queries=queries, sizes=sizes)
    own_book = (codebooks, None)

    def pieces(*arrays):
        return [(a, blocks_of(0, a.shape[0] // size)) for a in arrays]

    other_book, other_stretch = (y_pack, size), (y_pack, size + half * codes)

    state = call([(0, own_book, pieces(pack, x_pack, z_one[-1]), False)], stretch=None, state=None, final=False)
    *z_one, diag, first, second, third = lax.optimization_barrier((*z_one, diag, *state))
    state = (first, second, third)
    z_two, reached = [], [z_one[0]]
    for i, bits in enumerate(steps[1:]):
        z_two.append(along(reached, bits))
        reached = reached + [z_one[i + 1], z_two[-1]]
    diag_far = [along([diag], steps[0])]
    near = jnp.concatenate(z_one, axis=0)
    x_near, y_near = swap(near, 2), swap(near, 0, 1)
    state = call(
        [
            (0, own_book, pieces(*z_one[:-1]), True),
            (half, other_book, [(y_pack, blocks_of(0))] + pieces(diag), False),
        ],
        stretch=(*other_stretch, (1,)), state=state, final=False,
    )

    z_rest = jnp.concatenate(z_two, axis=0) if len(z_two) > 1 else z_two[0]
    x_rest, y_rest = swap(z_rest, 2), swap(z_rest, 0, 1)
    diag_far[0], first, second, third = lax.optimization_barrier((diag_far[0], *state))
    state = (first, second, third)
    for bits in steps[1:]:
        diag_far.append(along([diag] + diag_far, bits))
    state = call(
        [
            (0, own_book, pieces(z_rest, x_near), True),
            (half, other_book, pieces(diag_far[0], y_near), True),
        ],
        stretch=(*other_stretch, (0,)), state=state, final=False,
    )
    out, out_send = call(
        [(0, own_book, pieces(x_rest), True), (half, other_book, pieces(*diag_far[1:], y_rest), True)],
        stretch=None, state=state, final=True,
    )
    out_mate = swap(out_send, 1)
    return lay_out(place, out_mate, True, lay_out(place, out, False, None))


def rotate(tensor, position):
    half_dim = tensor.shape[-1] // 2
    ladder = jnp.arange(half_dim, dtype=jnp.float32)
    inverse = jnp.exp(ladder * jnp.float32(-2.0 * math.log(rope_base) / tensor.shape[-1]))
    angles = position.astype(jnp.float32)[:, None] * inverse[None, :]
    target = (position.shape[0],) + (1,) * (tensor.ndim - 2) + (half_dim,)
    cosine = jnp.cos(angles).reshape(target)
    sine_part = jnp.sin(angles).reshape(target)
    floats = tensor.astype(jnp.float32)
    first_half = floats[..., :half_dim]
    second_half = floats[..., half_dim:]
    return jnp.concatenate(
        [
            first_half * cosine - second_half * sine_part,
            second_half * cosine + first_half * sine_part,
        ],
        axis=-1,
    )


def decode_block(key_codes, codebooks):
    block_rows, kv_local, group_count = key_codes.shape
    entries = codebooks.shape[1]
    head_dim = codebooks.shape[2]
    ladder = lax.broadcasted_iota(jnp.int32, (1, 1, 1, entries), 3).astype(jnp.float32)
    one_hot = (key_codes.astype(jnp.float32)[..., None] == ladder).astype(jnp.bfloat16)
    code_table = codebooks.reshape(kv_local, entries, group_count, head_dim // group_count)
    decoded = jnp.einsum("bkgc,kcgd->bkgd", one_hot, code_table, preferred_element_type=jnp.float32)
    return decoded.reshape(block_rows, kv_local, head_dim)


def span_of():
    return 1024


def absorb(state, queries, key_rows, value_rows, allowed):
    running_max, running_sum, weighted = state
    scores = jnp.einsum(
        "tkgd,nkd->tkgn", queries, key_rows, preferred_element_type=jnp.float32
    ) * queries.shape[-1] ** (-0.5)
    if allowed is not None:
        scores = jnp.where(allowed[:, None, None, :], scores, -jnp.inf)
    new_max = jnp.maximum(running_max, jnp.max(scores, axis=-1))
    decay_factor = jnp.exp(running_max - new_max)
    weights = jnp.exp(scores - new_max[..., None])
    running_sum = running_sum * decay_factor + jnp.sum(weights, axis=-1)
    weighted = weighted * decay_factor[..., None] + jnp.einsum(
        "tkgn,nkd->tkgd",
        weights.astype(jnp.bfloat16),
        value_rows,
        preferred_element_type=jnp.float32,
    )
    return (new_max, running_sum, weighted)


def shards(qkv, key_codes, codebooks, value_codes, value_scales, block_ids):
    group_heads = qkv.shape[2] - 2
    head_dim = qkv.shape[3]
    block_rows = key_codes.shape[0]
    prefix_len = block_rows * lax.axis_size("outer")
    prefix_values = (value_codes.astype(jnp.float32) * value_scales[:, :, None]).astype(
        jnp.bfloat16
    )
    exchanged = lax.all_to_all(qkv, "inner", split_axis=1, concat_axis=0, tiled=True)
    stretch_rows = exchanged.shape[0]
    kv_local = exchanged.shape[1]
    local_pos = jnp.arange(stretch_rows, dtype=jnp.int32)
    stretch_pos = prefix_len + local_pos
    queries = rotate(exchanged[:, :, :group_heads, :], stretch_pos).astype(jnp.bfloat16)
    stretch_keys = rotate(exchanged[:, :, group_heads, :], stretch_pos).astype(jnp.bfloat16)
    stretch_values = exchanged[:, :, group_heads + 1, :]
    initial = (
        jnp.full((stretch_rows, kv_local, group_heads), -1e30, jnp.float32),
        jnp.zeros((stretch_rows, kv_local, group_heads), jnp.float32),
        jnp.zeros((stretch_rows, kv_local, group_heads, head_dim), jnp.float32),
    )
    own_pos = block_ids[0] * block_rows + jnp.arange(block_rows, dtype=jnp.int32)
    prefix_keys = rotate(decode_block(key_codes, codebooks), own_pos).astype(jnp.bfloat16)
    key_rows = lax.all_gather(prefix_keys, "outer", axis=0, tiled=True)
    value_rows = lax.all_gather(prefix_values, "outer", axis=0, tiled=True)
    length = key_rows.shape[0]
    span_rows = span_of()

    def advance(step_index, inner_state):
        first_row = step_index * span_rows
        key_part = lax.dynamic_slice_in_dim(key_rows, first_row, span_rows, 0)
        value_part = lax.dynamic_slice_in_dim(value_rows, first_row, span_rows, 0)
        return absorb(inner_state, queries, key_part, value_part, None)

    allowed = local_pos[None, :] <= local_pos[:, None]
    final_state = lax.fori_loop(
        0,
        length // span_rows,
        advance,
        absorb(initial, queries, stretch_keys, stretch_values, allowed),
    )
    running_max, running_sum, weighted = final_state
    outputs = (weighted / running_sum[..., None]).astype(jnp.bfloat16)
    return lax.all_to_all(outputs, "inner", split_axis=0, concat_axis=1, tiled=True)


def solution(mesh):
    n_outer, n_inner = mesh.shape["outer"], mesh.shape["inner"]

    def body(qkv, key_codes, codebooks, value_codes, value_scales, block_ids):
        arrays = (qkv, key_codes, codebooks, value_codes, value_scales, block_ids)
        head_dim = qkv.shape[3]
        far = n_outer // 4
        fits = (
            n_inner == 2
            and n_outer % 4 == 0
            and 4 <= far
            and far & (far - 1) == 0
            and n_outer <= 128
            and key_codes.shape[1] % 2 == 0
            and key_codes.shape[0] == 128
            and head_dim == 128
            and head_dim // key_codes.shape[2] == 8
            and key_codes.shape[2] % 16 == 0
            and codebooks.shape[1] % 128 == 0
            and qkv.shape[2] == 10
            and qkv.shape[0] % 32 == 0
        )
        if fits:
            return paired(*arrays, n_outer=n_outer)
        return shards(*arrays)

    return jax.shard_map(
        body,
        mesh=mesh,
        in_specs=(
            P(("outer", "inner"), None, None, None),
            P("outer", "inner", None),
            P("inner", None, None),
            P("outer", "inner", None),
            P("outer", "inner"),
            P("outer"),
        ),
        out_specs=P(("outer", "inner"), None, None, None),
        check_vma=False,
    )
```

```python
import functools
import math

import jax
import jax.numpy as jnp
import numpy as np
from jax import lax
from jax.experimental import pallas as pl
from jax.experimental.pallas import tpu as pltpu
from jax.sharding import PartitionSpec as P

rope_base = 500000.0
axes = ("outer", "inner")
bf16 = jnp.bfloat16
f32 = jnp.float32


def frequencies(head_dim):
    ladder = np.arange(head_dim // 2, dtype=np.float32)
    return np.exp(ladder * np.float32(-2.0 * math.log(rope_base) / head_dim)).astype(np.float32)


def angle_table(positions, head_dim):
    return frequencies(head_dim)[:, None] * positions.astype(np.float32)[None, :]


def whole(memory=pltpu.VMEM):
    return pl.BlockSpec(memory_space=memory)


def params(megabytes=16):
    return pltpu.CompilerParams(vmem_limit_bytes=megabytes * 2**20)


def prepare(place, ids, codes, values, scales, qkv, prefix, half):
    rows, kv_local, groups = codes.shape
    tokens, n_heads, slots, head_dim = qkv.shape
    group = slots - 2
    q_rows = tokens * group
    extent = half * (rows + groups)
    n_out = 2 * half
    kv_at = extent + 16 + n_out * q_rows
    size = kv_at + n_out * 2 * tokens
    angles = angle_table(np.arange(2 * tokens) + prefix, head_dim)
    cosine, sine = np.cos(angles).T, np.sin(angles).T
    cosine = jnp.asarray(np.concatenate([cosine, cosine], axis=1).astype(np.float32))
    sine = jnp.asarray(np.concatenate([-sine, sine], axis=1).astype(np.float32))
    sources = (codes.transpose(1, 2, 0), values, scales.T, qkv.transpose(0, 2, 1, 3), cosine, sine)

    def kernel(place, ids, *refs):
        given, (keep, send), held = refs[:6], refs[6:8], refs[8:14]
        codes, values, scales, qkv, cosine, sine = held
        q_scratch, k_scratch, v_scratch, sems = refs[14:]
        core, inner = place[0], place[1]
        copies = [pltpu.make_async_copy(*pair, sems.at[i]) for i, pair in enumerate(zip(given, held))]
        for copy in copies:
            copy.start()
        for copy in copies[:3]:
            copy.wait()
        diagonal = lax.broadcasted_iota(jnp.int32, (rows, rows), 0) == lax.broadcasted_iota(jnp.int32, (rows, rows), 1)

        def put(target, head, k):
            factor = jnp.broadcast_to(scales[head : head + 1, :], (rows, rows))
            factor = jnp.sum(jnp.where(diagonal, factor, 0.0), axis=1, keepdims=True)
            target[k * rows : (k + 1) * rows, :] = (values[:, head, :].astype(f32) * factor).astype(bf16)
            first = half * rows + k * groups
            target[first : first + groups, :] = codes[head].astype(f32).astype(bf16)

        for side in range(2):

            @pl.when(core == side)
            def _():
                for k in range(half):
                    put(send, (1 - side) * half + k, k)
                    put(keep, side * half + k, k)

        number = jnp.full((16, head_dim), ids[0], jnp.int32).astype(f32).astype(bf16)
        send[extent : extent + 16, :] = number
        keep[extent : extent + 16, :] = number
        for copy in copies[3:]:
            copy.wait()
        at = pl.ds(pl.multiple_of(inner * tokens, tokens), tokens)
        cos, sin = cosine[at, :][:, None, :], sine[at, :][:, None, :]

        def turn(x):
            return x * cos + pltpu.roll(x, head_dim // 2, 2) * sin

        spread = (tokens, 1, n_heads, head_dim)
        for slot in range(group):
            x = turn(qkv[:, slot, :, :].astype(f32))
            q_scratch[:tokens, slot : slot + 1, :, :] = x.reshape(spread)
        k_scratch[:tokens] = turn(qkv[:, group, :, :].astype(f32))
        v_scratch[:tokens] = qkv[:, group + 1, :, :].astype(f32)
        q_flat = q_scratch.reshape((tokens + 1) * group * n_heads, head_dim)
        k_flat = k_scratch.reshape((tokens + 1) * n_heads, head_dim)
        v_flat = v_scratch.reshape((tokens + 1) * n_heads, head_dim)
        for target, which in ((send, 1 - core), (keep, core)):
            for j in range(n_out):
                head = (inner if j < half else 1 - inner) * kv_local + which * half + j % half
                first = extent + 16 + j * q_rows
                target[first : first + q_rows, :] = q_flat[pl.ds(head, q_rows, stride=n_heads), :].astype(bf16)
                first = kv_at + j * 2 * tokens
                target[first : first + tokens, :] = k_flat[pl.ds(head, tokens, stride=n_heads), :].astype(bf16)
                first += tokens
                target[first : first + tokens, :] = v_flat[pl.ds(head, tokens, stride=n_heads), :].astype(bf16)

    shape = jax.ShapeDtypeStruct((size, head_dim), bf16)
    return pl.pallas_call(
        kernel,
        out_shape=(shape, shape),
        in_specs=[whole(pltpu.SMEM)] * 2 + [whole(pltpu.HBM)] * 6,
        out_specs=(whole(), whole()),
        scratch_shapes=[pltpu.VMEM(x.shape, x.dtype) for x in sources]
        + [
            pltpu.VMEM((tokens + 1, group, n_heads, head_dim), f32),
            pltpu.VMEM((tokens + 1, n_heads, head_dim), f32),
            pltpu.VMEM((tokens + 1, n_heads, head_dim), f32),
            pltpu.SemaphoreType.DMA((6,)),
        ],
        compiler_params=params(),
        name="prepare",
    )(place, ids, *[pltpu.with_memory_space_constraint(x, pltpu.HBM) for x in sources])


def attend(place, groups_of, tables, queries, stretch, state, sizes, final, megabytes=32):
    half, rows, groups, tokens, group, head_dim, codes = sizes
    q_rows = tokens * group
    scale = head_dim**-0.5 * math.log2(math.e)
    gd = head_dim // groups
    half_dim = head_dim // 2
    n_heads = 2 * half
    q_at = half * (rows + groups) + 16
    kv_at = q_at + n_heads * q_rows
    lengths = [sum(len(blocks) for _, blocks in pieces) * rows for _, _, pieces, _ in groups_of]
    extra = 2 * tokens if stretch is not None else 0
    chunk = 256

    operands, where = [], {}

    def ref_of(array):
        if id(array) not in where:
            where[id(array)] = len(operands)
            operands.append(array)
        return where[id(array)]

    plan = [
        (first, ref_of(book), row, [(ref_of(array), blocks) for array, blocks in pieces])
        for first, (book, row), pieces, _ in groups_of
    ]
    table_at = [ref_of(t) for t in tables]
    query_at = [ref_of(q) for q in queries]
    stretch_at = ref_of(stretch[0]) if stretch is not None else None
    n_plain = len(operands)
    if state is not None:
        operands += list(state)

    def kernel(place, *refs):
        refs = list(refs)
        given = refs[:n_plain]
        before = refs[n_plain : n_plain + 3] if state is not None else None
        refs = refs[len(operands) :]
        results = refs[: 2 if final else 3]
        refs = refs[len(results) :]
        kts, vvs = refs[: len(plan)], refs[len(plan) : 2 * len(plan)]
        tab, slots = refs[2 * len(plan)], refs[2 * len(plan) + 1 :]
        core, inner = place[0], place[1]
        cos_tok, sin_tok, cos_blk, sin_blk = [given[i] for i in table_at]
        requests = [given[i] for i in query_at]
        other = given[stretch_at] if stretch is not None else None

        def load_books(group_index):
            first, book_at, book_row, pieces = plan[group_index]
            book = given[book_at]
            for k in range(half):
                if book_row is None:
                    entries = book[core * half + k]
                else:
                    entries = book[book_row + k * codes : book_row + (k + 1) * codes, :]
                tab[group_index * half + k] = entries.astype(f32).T

        def decode(group_index, index, at, value_row, code_row, id_row):
            kt, vv, ref = kts[group_index], vvs[group_index], given[at]
            base = id_row - id_row % 16
            block = ref[base : base + 16, :].astype(f32)
            block = block[id_row % 16 : id_row % 16 + 8].astype(jnp.int32)
            block = jnp.broadcast_to(block[None], (half_dim // 8, 8, head_dim)).reshape(half_dim, head_dim)
            cb = jnp.take_along_axis(cos_blk[...], block, axis=1, mode="promise_in_bounds")
            sb = jnp.take_along_axis(sin_blk[...], block, axis=1, mode="promise_in_bounds")
            ct, st = cos_tok[...], sin_tok[...]
            cos = cb * ct - sb * st
            sin = sb * ct + cb * st
            span = slice(index * rows, (index + 1) * rows)
            for k in range(half):
                table = group_index * half + k
                code = ref[code_row + k * groups : code_row + (k + 1) * groups, :].astype(f32).astype(jnp.int32)
                code = jnp.broadcast_to(code[:, None, :], (groups, gd, rows)).reshape(head_dim, rows)
                low = code & 127
                key = jnp.take_along_axis(tab[table, :, :128], low, axis=1, mode="promise_in_bounds")
                for part in range(1, codes // 128):
                    entries = tab[table, :, part * 128 : (part + 1) * 128]
                    more = jnp.take_along_axis(entries, low, axis=1, mode="promise_in_bounds")
                    key = jnp.where(code >= part * 128, more, key)
                a, b = key[:half_dim], key[half_dim:]
                key = jnp.concatenate([a * cos - b * sin, b * cos + a * sin], axis=0).astype(bf16)
                kt[k, :head_dim, span] = key
                kt[k, head_dim:, span] = key
                vv[k, span, :] = ref[value_row + k * rows : value_row + (k + 1) * rows, :]

        def blocks_in(group_index):
            every = [(at, *block) for at, blocks in plan[group_index][3] for block in blocks]
            return [functools.partial(decode, group_index, i, *block) for i, block in enumerate(every)]

        for group_index in range(len(plan)):
            load_books(group_index)
        for task in blocks_in(0):
            task()
        later = blocks_in(1) if len(plan) > 1 else []

        works = [(g, k) for g in range(len(plan)) for k in range(half)]

        def parts(work):
            return [(c, min(chunk, lengths[work[0]] - c)) for c in range(0, lengths[work[0]], chunk)]

        def scaled_queries(work):
            g, k = work
            first = q_at + (plan[g][0] + k) * q_rows
            scaled = jnp.concatenate([ref[first : first + q_rows, :] for ref in requests], axis=0).astype(f32) * scale
            hi = scaled.astype(bf16)
            lo = (scaled - hi.astype(f32)).astype(bf16)
            return jnp.concatenate([hi, lo], axis=1)

        def fold(top, score):
            for i in range(score.shape[1] // 128):
                piece = score[:, i * 128 : (i + 1) * 128]
                top = piece if top is None else jnp.maximum(top, piece)
            return top

        def score_part(work, q, slot, top, c, width):
            score = jnp.dot(q, kts[work[0]][work[1], :, c : c + width], preferred_element_type=f32)
            slot[:, c : c + width] = score
            return fold(top, score)

        def stretch_rows(work, e, which):
            g, k = work
            head = plan[g][0] + k
            base = stretch[1] + (e * n_heads + (head + half) % n_heads) * 2 * tokens + which * tokens
            mine = kv_at + head * 2 * tokens + which * tokens
            return jnp.concatenate([other[base : base + tokens, :], requests[e][mine : mine + tokens, :]], axis=0)

        def score_stretch(work, q, slot, top):
            for e in range(2):
                key = stretch_rows(work, e, 0)
                key = jnp.concatenate([key, key], axis=1)
                score = lax.dot_general(
                    q[e * q_rows : (e + 1) * q_rows], key, (((1,), (1,)), ((), ())), preferred_element_type=f32
                )
                column = lax.broadcasted_iota(jnp.int32, score.shape, 1)
                row = lax.broadcasted_iota(jnp.int32, score.shape, 0) // group
                allowed = (column - tokens <= row) & (column >= tokens * (1 - inner))
                tops.append(jnp.where(allowed, score, -jnp.inf))
                slot[e * q_rows : (e + 1) * q_rows, lengths[work[0]] : lengths[work[0]] + extra] = tops[-1]
            return fold(top, jnp.concatenate(tops[-2:], axis=0))

        tops = []

        def weigh(slot, m, part, mixed, c, width, value):
            weights = []
            for i in range(c, c + width, 128):
                weight = jnp.exp2(slot[:, i : i + 128] - m)
                part = part + weight
                weights.append(weight.astype(bf16))
            weight = jnp.concatenate(weights, axis=1) if len(weights) > 1 else weights[0]
            if isinstance(value, list):
                new = [jnp.dot(weight[i * q_rows : (i + 1) * q_rows], v, preferred_element_type=f32) for i, v in enumerate(value)]
                return part, mixed + jnp.concatenate(new, axis=0)
            return part, mixed + jnp.dot(weight, value, preferred_element_type=f32)

        def place_of(work):
            g, k = work
            return plan[g][0] + k

        current = None
        for t in range(len(works) + 1):
            slot, old = slots[t % 2], slots[1 - t % 2]
            work = works[t] if t < len(works) else None
            top = None
            if work is not None:
                q = scaled_queries(work)
            if current is not None:
                done, m, part, mixed = current
            if stretch is not None:
                if work is not None and work[0] in stretch[2]:
                    top = score_stretch(work, q, slot, top)
                if current is not None and done[0] in stretch[2]:
                    part, mixed = weigh(old, m, part, mixed, lengths[done[0]], extra, [stretch_rows(done, e, 1) for e in range(2)])
            ahead = parts(work) if work is not None else []
            behind = parts(done) if current is not None else []
            first_steps = half * len(parts(works[0]))
            for i in range(max(len(ahead), len(behind))):
                for _ in range(-(-len(blocks_in(1)) // first_steps) if later else 0):
                    if later:
                        later.pop(0)()
                if i < len(ahead):
                    top = score_part(work, q, slot, top, *ahead[i])
                if i < len(behind):
                    c, width = behind[i]
                    part, mixed = weigh(old, m, part, mixed, c, width, vvs[done[0]][done[1], c : c + width, :])
            if current is not None:
                if final:
                    head = plan[done[0]][0] + done[1]
                    result = mixed / jnp.sum(part, axis=1, keepdims=True)
                    for e in range(2):
                        result_e = result[e * q_rows : (e + 1) * q_rows].reshape(tokens, group, head_dim)
                        results[e][head] = result_e.astype(bf16)
                else:
                    for ref, value in zip(results, (m, part, mixed)):
                        ref[place_of(done)] = value
            if work is not None:
                m = jnp.broadcast_to(jnp.max(top, axis=1, keepdims=True), (2 * q_rows, 128))
                if not groups_of[work[0]][3]:
                    part = jnp.zeros((2 * q_rows, 128), f32)
                    mixed = jnp.zeros((2 * q_rows, head_dim), f32)
                else:
                    past = before[0][place_of(work)]
                    m = jnp.maximum(past, m)
                    decay = jnp.exp2(past - m)
                    part = before[1][place_of(work)] * decay
                    mixed = before[2][place_of(work)] * decay
                current = (work, m, part, mixed)

    if final:
        out_shape = (jax.ShapeDtypeStruct((n_heads, tokens, group, head_dim), bf16),) * 2
    else:
        out_shape = (jax.ShapeDtypeStruct((n_heads, 2 * q_rows, 128), f32),) * 3
    alias = {1 + n_plain + j: j for j in range(3)} if state is not None and not final else {}
    pairs = 2 * half * q_rows * (sum(lengths) + (extra * len(stretch[2]) if stretch is not None else 0))
    slot = pltpu.VMEM((2 * q_rows, max(lengths) + extra), f32)
    return pl.pallas_call(
        kernel,
        out_shape=out_shape,
        in_specs=[whole(pltpu.SMEM)] + [whole() for _ in operands],
        out_specs=(whole(),) * len(out_shape),
        scratch_shapes=[pltpu.VMEM((half, 2 * head_dim, n), bf16) for n in lengths]
        + [pltpu.VMEM((half, n, head_dim), bf16) for n in lengths]
        + [pltpu.VMEM((len(lengths) * half, head_dim, codes), f32), slot, slot],
        input_output_aliases=alias,
        compiler_params=params(megabytes),
        cost_estimate=pl.CostEstimate(flops=8 * pairs * head_dim, bytes_accessed=4 * 2**20, transcendentals=pairs),
        name="attend",
    )(place, *operands)


def lay_out(place, heads_of, foreign, out):
    n_out, tokens, group, head_dim = heads_of.shape
    half = n_out // 2

    def kernel(place, source, *refs):
        target, sems = refs[-2:]
        core, inner = place[0], place[1]
        which = 1 - core if foreign else core
        copies = []
        for j in range(n_out):
            head = (inner if j < half else 1 - inner) * n_out + which * half + j % half
            copies.append(pltpu.make_async_copy(source.at[j], target.at[:, head], sems.at[j]))
            copies[-1].start()
        for copy in copies:
            copy.wait()

    return pl.pallas_call(
        kernel,
        out_shape=jax.ShapeDtypeStruct((tokens, 2 * n_out, group, head_dim), bf16),
        in_specs=[whole(pltpu.SMEM), whole()] + ([] if out is None else [whole(pl.ANY)]),
        out_specs=whole(pl.ANY),
        scratch_shapes=[pltpu.SemaphoreType.DMA((n_out,))],
        input_output_aliases={} if out is None else {2: 0},
        compiler_params=params(),
        name="lay_out",
    )(place, heads_of, *([] if out is None else [out]))


def paired(qkv, key_codes, codebooks, value_codes, value_scales, block_ids, *, n_outer):
    tokens, n_heads, slots, head_dim = qkv.shape
    group = slots - 2
    rows, kv_local, groups = key_codes.shape
    codes = codebooks.shape[1]
    half = kv_local // 2
    n_far = n_outer // 4
    prefix = rows * n_outer
    outer, inner = lax.axis_index("outer"), lax.axis_index("inner")
    core = outer % 2
    place = jnp.stack([core, inner]).astype(jnp.int32)
    extent = half * (rows + groups)

    def swap(x, outer_bits, inner_bits=0):
        return lax.ppermute(
            x,
            axes,
            [
                (2 * o + i, 2 * (o ^ outer_bits) + (i ^ inner_bits))
                for o in range(n_outer)
                for i in range(2)
            ],
        )

    keep, send = prepare(place, block_ids, key_codes, value_codes, value_scales, qkv, prefix, half)
    mate = swap(send, 1)
    queries = (keep, mate)

    pack = jnp.concatenate([keep[:extent], mate[:extent], keep[extent : extent + 8], mate[extent : extent + 8]], axis=0)
    size = pack.shape[0]

    def blocks_of(base, count=1):
        out = []
        for j in range(count):
            b = base + j * size
            out.append((b, b + half * rows, b + 2 * extent))
            out.append((b + extent, b + extent + half * rows, b + 2 * extent + 8))
        return out

    my_books = lax.dynamic_slice_in_dim(codebooks, core * half, half, 0).reshape(half * codes, head_dim)
    own_kv = 2 * half * 2 * tokens
    stretch = jnp.concatenate([keep[-own_kv:], mate[-own_kv:]], axis=0)

    def along(parts, bits):
        return swap(jnp.concatenate(parts, axis=0) if len(parts) > 1 else parts[0], 4 * bits)

    steps = [n_far >> (i + 1) for i in range(n_far.bit_length() - 1)]
    z_one = [along([pack], bits) for bits in steps]
    x_pack = swap(pack, 2)
    y_pack = swap(jnp.concatenate([pack, my_books, stretch], axis=0), 0, 1)
    diag = swap(pack, 2, 1)

    positions = np.arange(rows)
    cos_tok, sin_tok = np.cos(angle_table(positions, head_dim)), np.sin(angle_table(positions, head_dim))
    starts = np.arange(128) * rows
    cos_blk, sin_blk = np.cos(angle_table(starts, head_dim)), np.sin(angle_table(starts, head_dim))
    tables = [jnp.asarray(t.astype(np.float32)) for t in (cos_tok, sin_tok, cos_blk, sin_blk)]
    sizes = (half, rows, groups, tokens, group, head_dim, codes)
    call = functools.partial(attend, place, tables=tables, queries=queries, sizes=sizes)
    own_book = (codebooks, None)

    def pieces(*arrays):
        return [(a, blocks_of(0, a.shape[0] // size)) for a in arrays]

    other_book, other_stretch = (y_pack, size), (y_pack, size + half * codes)

    state = call([(0, own_book, pieces(pack, x_pack, z_one[-1]), False)], stretch=None, state=None, final=False)
    *z_one, diag, first, second, third = lax.optimization_barrier((*z_one, diag, *state))
    state = (first, second, third)
    z_two, reached = [], [z_one[0]]
    for i, bits in enumerate(steps[1:]):
        z_two.append(along(reached, bits))
        reached = reached + [z_one[i + 1], z_two[-1]]
    diag_far = [along([diag], steps[0])]
    near = jnp.concatenate(z_one, axis=0)
    x_near, y_near = swap(near, 2), swap(near, 0, 1)
    state = call(
        [
            (0, own_book, pieces(*z_one[:-1]), True),
            (half, other_book, [(y_pack, blocks_of(0))] + pieces(diag), False),
        ],
        stretch=(*other_stretch, (1,)), state=state, final=False,
    )

    z_rest = jnp.concatenate(z_two, axis=0) if len(z_two) > 1 else z_two[0]
    x_rest, y_rest = swap(z_rest, 2), swap(z_rest, 0, 1)
    diag_far[0], first, second, third = lax.optimization_barrier((diag_far[0], *state))
    state = (first, second, third)
    for bits in steps[1:]:
        diag_far.append(along([diag] + diag_far, bits))
    state = call(
        [
            (0, own_book, pieces(z_rest, x_near), True),
            (half, other_book, pieces(diag_far[0], y_near), True),
        ],
        stretch=(*other_stretch, (0,)), state=state, final=False,
    )
    out, out_send = call(
        [(0, own_book, pieces(x_rest), True), (half, other_book, pieces(*diag_far[1:], y_rest), True)],
        stretch=None, state=state, final=True,
    )
    out_mate = swap(out_send, 1)
    return lay_out(place, out_mate, True, lay_out(place, out, False, None))


def rotate(tensor, position):
    half_dim = tensor.shape[-1] // 2
    ladder = jnp.arange(half_dim, dtype=jnp.float32)
    inverse = jnp.exp(ladder * jnp.float32(-2.0 * math.log(rope_base) / tensor.shape[-1]))
    angles = position.astype(jnp.float32)[:, None] * inverse[None, :]
    target = (position.shape[0],) + (1,) * (tensor.ndim - 2) + (half_dim,)
    cosine = jnp.cos(angles).reshape(target)
    sine_part = jnp.sin(angles).reshape(target)
    floats = tensor.astype(jnp.float32)
    first_half = floats[..., :half_dim]
    second_half = floats[..., half_dim:]
    return jnp.concatenate(
        [
            first_half * cosine - second_half * sine_part,
            second_half * cosine + first_half * sine_part,
        ],
        axis=-1,
    )


def decode_block(key_codes, codebooks):
    block_rows, kv_local, group_count = key_codes.shape
    entries = codebooks.shape[1]
    head_dim = codebooks.shape[2]
    ladder = lax.broadcasted_iota(jnp.int32, (1, 1, 1, entries), 3).astype(jnp.float32)
    one_hot = (key_codes.astype(jnp.float32)[..., None] == ladder).astype(jnp.bfloat16)
    code_table = codebooks.reshape(kv_local, entries, group_count, head_dim // group_count)
    decoded = jnp.einsum("bkgc,kcgd->bkgd", one_hot, code_table, preferred_element_type=jnp.float32)
    return decoded.reshape(block_rows, kv_local, head_dim)


def span_of():
    return 1024


def absorb(state, queries, key_rows, value_rows, allowed):
    running_max, running_sum, weighted = state
    scores = jnp.einsum(
        "tkgd,nkd->tkgn", queries, key_rows, preferred_element_type=jnp.float32
    ) * queries.shape[-1] ** (-0.5)
    if allowed is not None:
        scores = jnp.where(allowed[:, None, None, :], scores, -jnp.inf)
    new_max = jnp.maximum(running_max, jnp.max(scores, axis=-1))
    decay_factor = jnp.exp(running_max - new_max)
    weights = jnp.exp(scores - new_max[..., None])
    running_sum = running_sum * decay_factor + jnp.sum(weights, axis=-1)
    weighted = weighted * decay_factor[..., None] + jnp.einsum(
        "tkgn,nkd->tkgd",
        weights.astype(jnp.bfloat16),
        value_rows,
        preferred_element_type=jnp.float32,
    )
    return (new_max, running_sum, weighted)


def shards(qkv, key_codes, codebooks, value_codes, value_scales, block_ids):
    group_heads = qkv.shape[2] - 2
    head_dim = qkv.shape[3]
    block_rows = key_codes.shape[0]
    prefix_len = block_rows * lax.axis_size("outer")
    prefix_values = (value_codes.astype(jnp.float32) * value_scales[:, :, None]).astype(
        jnp.bfloat16
    )
    exchanged = lax.all_to_all(qkv, "inner", split_axis=1, concat_axis=0, tiled=True)
    stretch_rows = exchanged.shape[0]
    kv_local = exchanged.shape[1]
    local_pos = jnp.arange(stretch_rows, dtype=jnp.int32)
    stretch_pos = prefix_len + local_pos
    queries = rotate(exchanged[:, :, :group_heads, :], stretch_pos).astype(jnp.bfloat16)
    stretch_keys = rotate(exchanged[:, :, group_heads, :], stretch_pos).astype(jnp.bfloat16)
    stretch_values = exchanged[:, :, group_heads + 1, :]
    initial = (
        jnp.full((stretch_rows, kv_local, group_heads), -1e30, jnp.float32),
        jnp.zeros((stretch_rows, kv_local, group_heads), jnp.float32),
        jnp.zeros((stretch_rows, kv_local, group_heads, head_dim), jnp.float32),
    )
    own_pos = block_ids[0] * block_rows + jnp.arange(block_rows, dtype=jnp.int32)
    prefix_keys = rotate(decode_block(key_codes, codebooks), own_pos).astype(jnp.bfloat16)
    key_rows = lax.all_gather(prefix_keys, "outer", axis=0, tiled=True)
    value_rows = lax.all_gather(prefix_values, "outer", axis=0, tiled=True)
    length = key_rows.shape[0]
    span_rows = span_of()

    def advance(step_index, inner_state):
        first_row = step_index * span_rows
        key_part = lax.dynamic_slice_in_dim(key_rows, first_row, span_rows, 0)
        value_part = lax.dynamic_slice_in_dim(value_rows, first_row, span_rows, 0)
        return absorb(inner_state, queries, key_part, value_part, None)

    allowed = local_pos[None, :] <= local_pos[:, None]
    final_state = lax.fori_loop(
        0,
        length // span_rows,
        advance,
        absorb(initial, queries, stretch_keys, stretch_values, allowed),
    )
    running_max, running_sum, weighted = final_state
    outputs = (weighted / running_sum[..., None]).astype(jnp.bfloat16)
    return lax.all_to_all(outputs, "inner", split_axis=0, concat_axis=1, tiled=True)


def solution(mesh):
    n_outer, n_inner = mesh.shape["outer"], mesh.shape["inner"]

    def body(qkv, key_codes, codebooks, value_codes, value_scales, block_ids):
        arrays = (qkv, key_codes, codebooks, value_codes, value_scales, block_ids)
        head_dim = qkv.shape[3]
        far = n_outer // 4
        fits = (
            n_inner == 2
            and n_outer % 4 == 0
            and 4 <= far
            and far & (far - 1) == 0
            and n_outer <= 128
            and key_codes.shape[1] % 2 == 0
            and key_codes.shape[0] == 128
            and head_dim == 128
            and head_dim // key_codes.shape[2] == 8
            and key_codes.shape[2] % 16 == 0
            and codebooks.shape[1] % 128 == 0
            and qkv.shape[2] == 10
            and qkv.shape[0] % 32 == 0
        )
        if fits:
            return paired(*arrays, n_outer=n_outer)
        return shards(*arrays)

    return jax.shard_map(
        body,
        mesh=mesh,
        in_specs=(
            P(("outer", "inner"), None, None, None),
            P("outer", "inner", None),
            P("inner", None, None),
            P("outer", "inner", None),
            P("outer", "inner"),
            P("outer"),
        ),
        out_specs=P(("outer", "inner"), None, None, None),
        check_vma=False,
    )
```

```python
import functools
import math

import jax
import jax.numpy as jnp
import numpy as np
from jax import lax
from jax.experimental import pallas as pl
from jax.experimental.pallas import tpu as pltpu
from jax.sharding import PartitionSpec as P

rope_base = 500000.0
axes = ("outer", "inner")
bf16 = jnp.bfloat16
f32 = jnp.float32


def frequencies(head_dim):
    ladder = np.arange(head_dim // 2, dtype=np.float32)
    return np.exp(ladder * np.float32(-2.0 * math.log(rope_base) / head_dim)).astype(np.float32)


def angle_table(positions, head_dim):
    return frequencies(head_dim)[:, None] * positions.astype(np.float32)[None, :]


def whole(memory=pltpu.VMEM):
    return pl.BlockSpec(memory_space=memory)


def params(megabytes=16):
    return pltpu.CompilerParams(vmem_limit_bytes=megabytes * 2**20)


def prepare(place, ids, codes, values, scales, qkv, prefix, half):
    rows, kv_local, groups = codes.shape
    tokens, n_heads, slots, head_dim = qkv.shape
    group = slots - 2
    q_rows = tokens * group
    extent = half * (rows + groups)
    n_out = 2 * half
    kv_at = extent + 16 + n_out * q_rows
    size = kv_at + n_out * 2 * tokens
    angles = angle_table(np.arange(2 * tokens) + prefix, head_dim)
    cosine, sine = np.cos(angles).T, np.sin(angles).T
    cosine = jnp.asarray(np.concatenate([cosine, cosine], axis=1).astype(np.float32))
    sine = jnp.asarray(np.concatenate([-sine, sine], axis=1).astype(np.float32))
    sources = (codes.transpose(1, 2, 0), values, scales.T, qkv.transpose(0, 2, 1, 3), cosine, sine)

    def kernel(place, ids, *refs):
        given, (keep, send), held = refs[:6], refs[6:8], refs[8:14]
        codes, values, scales, qkv, cosine, sine = held
        q_scratch, k_scratch, v_scratch, sems = refs[14:]
        core, inner = place[0], place[1]
        copies = [pltpu.make_async_copy(*pair, sems.at[i]) for i, pair in enumerate(zip(given, held))]
        for copy in copies:
            copy.start()
        for copy in copies[:3]:
            copy.wait()
        diagonal = lax.broadcasted_iota(jnp.int32, (rows, rows), 0) == lax.broadcasted_iota(jnp.int32, (rows, rows), 1)

        def put(target, head, k):
            factor = jnp.broadcast_to(scales[head : head + 1, :], (rows, rows))
            factor = jnp.sum(jnp.where(diagonal, factor, 0.0), axis=1, keepdims=True)
            target[k * rows : (k + 1) * rows, :] = (values[:, head, :].astype(f32) * factor).astype(bf16)
            first = half * rows + k * groups
            target[first : first + groups, :] = codes[head].astype(f32).astype(bf16)

        for side in range(2):

            @pl.when(core == side)
            def _():
                for k in range(half):
                    put(send, (1 - side) * half + k, k)
                    put(keep, side * half + k, k)

        number = jnp.full((16, head_dim), ids[0], jnp.int32).astype(f32).astype(bf16)
        send[extent : extent + 16, :] = number
        keep[extent : extent + 16, :] = number
        for copy in copies[3:]:
            copy.wait()
        at = pl.ds(pl.multiple_of(inner * tokens, tokens), tokens)
        cos, sin = cosine[at, :][:, None, :], sine[at, :][:, None, :]

        def turn(x):
            return x * cos + pltpu.roll(x, head_dim // 2, 2) * sin

        spread = (tokens, 1, n_heads, head_dim)
        for slot in range(group):
            x = turn(qkv[:, slot, :, :].astype(f32))
            q_scratch[:tokens, slot : slot + 1, :, :] = x.reshape(spread)
        k_scratch[:tokens] = turn(qkv[:, group, :, :].astype(f32))
        v_scratch[:tokens] = qkv[:, group + 1, :, :].astype(f32)
        q_flat = q_scratch.reshape((tokens + 1) * group * n_heads, head_dim)
        k_flat = k_scratch.reshape((tokens + 1) * n_heads, head_dim)
        v_flat = v_scratch.reshape((tokens + 1) * n_heads, head_dim)
        for target, which in ((send, 1 - core), (keep, core)):
            for j in range(n_out):
                head = (inner if j < half else 1 - inner) * kv_local + which * half + j % half
                first = extent + 16 + j * q_rows
                target[first : first + q_rows, :] = q_flat[pl.ds(head, q_rows, stride=n_heads), :].astype(bf16)
                first = kv_at + j * 2 * tokens
                target[first : first + tokens, :] = k_flat[pl.ds(head, tokens, stride=n_heads), :].astype(bf16)
                first += tokens
                target[first : first + tokens, :] = v_flat[pl.ds(head, tokens, stride=n_heads), :].astype(bf16)

    shape = jax.ShapeDtypeStruct((size, head_dim), bf16)
    return pl.pallas_call(
        kernel,
        out_shape=(shape, shape),
        in_specs=[whole(pltpu.SMEM)] * 2 + [whole(pltpu.HBM)] * 6,
        out_specs=(whole(), whole()),
        scratch_shapes=[pltpu.VMEM(x.shape, x.dtype) for x in sources]
        + [
            pltpu.VMEM((tokens + 1, group, n_heads, head_dim), f32),
            pltpu.VMEM((tokens + 1, n_heads, head_dim), f32),
            pltpu.VMEM((tokens + 1, n_heads, head_dim), f32),
            pltpu.SemaphoreType.DMA((6,)),
        ],
        compiler_params=params(),
        name="prepare",
    )(place, ids, *[pltpu.with_memory_space_constraint(x, pltpu.HBM) for x in sources])


def attend(place, groups_of, tables, queries, stretch, state, sizes, final, megabytes=32):
    half, rows, groups, tokens, group, head_dim, codes = sizes
    q_rows = tokens * group
    scale = head_dim**-0.5 * math.log2(math.e)
    gd = head_dim // groups
    half_dim = head_dim // 2
    n_heads = 2 * half
    q_at = half * (rows + groups) + 16
    kv_at = q_at + n_heads * q_rows
    lengths = [sum(len(blocks) for _, blocks in pieces) * rows for _, _, pieces, _ in groups_of]
    extra = 2 * tokens if stretch is not None else 0
    chunk = 512

    operands, where = [], {}

    def ref_of(array):
        if id(array) not in where:
            where[id(array)] = len(operands)
            operands.append(array)
        return where[id(array)]

    plan = [
        (first, ref_of(book), row, [(ref_of(array), blocks) for array, blocks in pieces])
        for first, (book, row), pieces, _ in groups_of
    ]
    table_at = [ref_of(t) for t in tables]
    query_at = [ref_of(q) for q in queries]
    stretch_at = ref_of(stretch[0]) if stretch is not None else None
    n_plain = len(operands)
    if state is not None:
        operands += list(state)

    def kernel(place, *refs):
        refs = list(refs)
        given = refs[:n_plain]
        before = refs[n_plain : n_plain + 3] if state is not None else None
        refs = refs[len(operands) :]
        results = refs[: 2 if final else 3]
        refs = refs[len(results) :]
        kts, vvs = refs[: len(plan)], refs[len(plan) : 2 * len(plan)]
        tab, slots = refs[2 * len(plan)], refs[2 * len(plan) + 1 :]
        core, inner = place[0], place[1]
        cos_tok, sin_tok, cos_blk, sin_blk = [given[i] for i in table_at]
        requests = [given[i] for i in query_at]
        other = given[stretch_at] if stretch is not None else None

        def load_books(group_index):
            first, book_at, book_row, pieces = plan[group_index]
            book = given[book_at]
            for k in range(half):
                if book_row is None:
                    entries = book[core * half + k]
                else:
                    entries = book[book_row + k * codes : book_row + (k + 1) * codes, :]
                tab[group_index * half + k] = entries.astype(f32).T

        def decode(group_index, index, at, value_row, code_row, id_row):
            kt, vv, ref = kts[group_index], vvs[group_index], given[at]
            base = id_row - id_row % 16
            block = ref[base : base + 16, :].astype(f32)
            block = block[id_row % 16 : id_row % 16 + 8].astype(jnp.int32)
            block = jnp.broadcast_to(block[None], (half_dim // 8, 8, head_dim)).reshape(half_dim, head_dim)
            cb = jnp.take_along_axis(cos_blk[...], block, axis=1, mode="promise_in_bounds")
            sb = jnp.take_along_axis(sin_blk[...], block, axis=1, mode="promise_in_bounds")
            ct, st = cos_tok[...], sin_tok[...]
            cos = cb * ct - sb * st
            sin = sb * ct + cb * st
            span = slice(index * rows, (index + 1) * rows)
            for k in range(half):
                table = group_index * half + k
                code = ref[code_row + k * groups : code_row + (k + 1) * groups, :].astype(f32).astype(jnp.int32)
                code = jnp.broadcast_to(code[:, None, :], (groups, gd, rows)).reshape(head_dim, rows)
                low = code & 127
                key = jnp.take_along_axis(tab[table, :, :128], low, axis=1, mode="promise_in_bounds")
                for part in range(1, codes // 128):
                    entries = tab[table, :, part * 128 : (part + 1) * 128]
                    more = jnp.take_along_axis(entries, low, axis=1, mode="promise_in_bounds")
                    key = jnp.where(code >= part * 128, more, key)
                a, b = key[:half_dim], key[half_dim:]
                key = jnp.concatenate([a * cos - b * sin, b * cos + a * sin], axis=0).astype(bf16)
                kt[k, :head_dim, span] = key
                kt[k, head_dim:, span] = key
                vv[k, span, :] = ref[value_row + k * rows : value_row + (k + 1) * rows, :]

        def blocks_in(group_index):
            every = [(at, *block) for at, blocks in plan[group_index][3] for block in blocks]
            return [functools.partial(decode, group_index, i, *block) for i, block in enumerate(every)]

        for group_index in range(len(plan)):
            load_books(group_index)
        for task in blocks_in(0):
            task()
        later = blocks_in(1) if len(plan) > 1 else []

        works = [(g, k, e) for g in range(len(plan)) for k in range(half) for e in range(2)]

        def parts(work):
            return [(c, min(chunk, lengths[work[0]] - c)) for c in range(0, lengths[work[0]], chunk)]

        def scaled_queries(work):
            g, k, e = work
            first = q_at + (plan[g][0] + k) * q_rows
            scaled = requests[e][first : first + q_rows, :].astype(f32) * scale
            hi = scaled.astype(bf16)
            lo = (scaled - hi.astype(f32)).astype(bf16)
            return jnp.concatenate([hi, lo], axis=1)

        def fold(top, score):
            for i in range(score.shape[1] // 128):
                piece = score[:, i * 128 : (i + 1) * 128]
                top = piece if top is None else jnp.maximum(top, piece)
            return top

        def score_part(work, q, slot, top, c, width):
            score = jnp.dot(q, kts[work[0]][work[1], :, c : c + width], preferred_element_type=f32)
            slot[:, c : c + width] = score
            return fold(top, score)

        def stretch_rows(work, which):
            g, k, e = work
            head = plan[g][0] + k
            base = stretch[1] + (e * n_heads + (head + half) % n_heads) * 2 * tokens + which * tokens
            mine = kv_at + head * 2 * tokens + which * tokens
            return jnp.concatenate([other[base : base + tokens, :], requests[e][mine : mine + tokens, :]], axis=0)

        def score_stretch(work, q, slot, top):
            key = stretch_rows(work, 0)
            key = jnp.concatenate([key, key], axis=1)
            score = lax.dot_general(q, key, (((1,), (1,)), ((), ())), preferred_element_type=f32)
            column = lax.broadcasted_iota(jnp.int32, score.shape, 1)
            row = lax.broadcasted_iota(jnp.int32, score.shape, 0) // group
            allowed = (column - tokens <= row) & (column >= tokens * (1 - inner))
            score = jnp.where(allowed, score, -jnp.inf)
            slot[:, lengths[work[0]] : lengths[work[0]] + extra] = score
            return fold(top, score)

        def weigh(slot, m, part, mixed, c, width, value):
            weights = []
            for i in range(c, c + width, 128):
                weight = jnp.exp2(slot[:, i : i + 128] - m)
                part = part + weight
                weights.append(weight.astype(bf16))
            weight = jnp.concatenate(weights, axis=1) if len(weights) > 1 else weights[0]
            return part, mixed + jnp.dot(weight, value, preferred_element_type=f32)

        def place_of(work):
            g, k, e = work
            return plan[g][0] + k, slice(e * q_rows, (e + 1) * q_rows), slice(None)

        current = None
        for t in range(len(works) + 1):
            slot, old = slots[t % 2], slots[1 - t % 2]
            work = works[t] if t < len(works) else None
            top = None
            if work is not None:
                q = scaled_queries(work)
            if current is not None:
                done, m, part, mixed = current
            if stretch is not None:
                if work is not None and work[0] in stretch[2]:
                    top = score_stretch(work, q, slot, top)
                if current is not None and done[0] in stretch[2]:
                    part, mixed = weigh(old, m, part, mixed, lengths[done[0]], extra, stretch_rows(done, 1))
            ahead = parts(work) if work is not None else []
            behind = parts(done) if current is not None else []
            first_steps = 2 * half * len(parts(works[0]))
            for i in range(max(len(ahead), len(behind))):
                for _ in range(-(-len(blocks_in(1)) // first_steps) if later else 0):
                    if later:
                        later.pop(0)()
                if i < len(ahead):
                    top = score_part(work, q, slot, top, *ahead[i])
                if i < len(behind):
                    c, width = behind[i]
                    part, mixed = weigh(old, m, part, mixed, c, width, vvs[done[0]][done[1], c : c + width, :])
            if current is not None:
                if final:
                    head = plan[done[0]][0] + done[1]
                    result = mixed / jnp.sum(part, axis=1, keepdims=True)
                    results[done[2]][head] = result.reshape(tokens, group, head_dim).astype(bf16)
                else:
                    for ref, value in zip(results, (m, part, mixed)):
                        ref[place_of(done)] = value
            if work is not None:
                m = jnp.broadcast_to(jnp.max(top, axis=1, keepdims=True), (q_rows, 128))
                if not groups_of[work[0]][3]:
                    part = jnp.zeros((q_rows, 128), f32)
                    mixed = jnp.zeros((q_rows, head_dim), f32)
                else:
                    past = before[0][place_of(work)]
                    m = jnp.maximum(past, m)
                    decay = jnp.exp2(past - m)
                    part = before[1][place_of(work)] * decay
                    mixed = before[2][place_of(work)] * decay
                current = (work, m, part, mixed)

    if final:
        out_shape = (jax.ShapeDtypeStruct((n_heads, tokens, group, head_dim), bf16),) * 2
    else:
        out_shape = (jax.ShapeDtypeStruct((n_heads, 2 * q_rows, 128), f32),) * 3
    alias = {1 + n_plain + j: j for j in range(3)} if state is not None and not final else {}
    pairs = 2 * half * q_rows * (sum(lengths) + (extra * len(stretch[2]) if stretch is not None else 0))
    slot = pltpu.VMEM((q_rows, max(lengths) + extra), f32)
    return pl.pallas_call(
        kernel,
        out_shape=out_shape,
        in_specs=[whole(pltpu.SMEM)] + [whole() for _ in operands],
        out_specs=(whole(),) * len(out_shape),
        scratch_shapes=[pltpu.VMEM((half, 2 * head_dim, n), bf16) for n in lengths]
        + [pltpu.VMEM((half, n, head_dim), bf16) for n in lengths]
        + [pltpu.VMEM((len(lengths) * half, head_dim, codes), f32), slot, slot],
        input_output_aliases=alias,
        compiler_params=params(megabytes),
        cost_estimate=pl.CostEstimate(flops=8 * pairs * head_dim, bytes_accessed=4 * 2**20, transcendentals=pairs),
        name="attend",
    )(place, *operands)


def lay_out(place, heads_of, foreign, out):
    n_out, tokens, group, head_dim = heads_of.shape
    half = n_out // 2

    def kernel(place, source, *refs):
        target, sems = refs[-2:]
        core, inner = place[0], place[1]
        which = 1 - core if foreign else core
        copies = []
        for j in range(n_out):
            head = (inner if j < half else 1 - inner) * n_out + which * half + j % half
            copies.append(pltpu.make_async_copy(source.at[j], target.at[:, head], sems.at[j]))
            copies[-1].start()
        for copy in copies:
            copy.wait()

    return pl.pallas_call(
        kernel,
        out_shape=jax.ShapeDtypeStruct((tokens, 2 * n_out, group, head_dim), bf16),
        in_specs=[whole(pltpu.SMEM), whole()] + ([] if out is None else [whole(pl.ANY)]),
        out_specs=whole(pl.ANY),
        scratch_shapes=[pltpu.SemaphoreType.DMA((n_out,))],
        input_output_aliases={} if out is None else {2: 0},
        compiler_params=params(),
        name="lay_out",
    )(place, heads_of, *([] if out is None else [out]))


def paired(qkv, key_codes, codebooks, value_codes, value_scales, block_ids, *, n_outer):
    tokens, n_heads, slots, head_dim = qkv.shape
    group = slots - 2
    rows, kv_local, groups = key_codes.shape
    codes = codebooks.shape[1]
    half = kv_local // 2
    n_far = n_outer // 4
    prefix = rows * n_outer
    outer, inner = lax.axis_index("outer"), lax.axis_index("inner")
    core = outer % 2
    place = jnp.stack([core, inner]).astype(jnp.int32)
    extent = half * (rows + groups)

    def swap(x, outer_bits, inner_bits=0):
        return lax.ppermute(
            x,
            axes,
            [
                (2 * o + i, 2 * (o ^ outer_bits) + (i ^ inner_bits))
                for o in range(n_outer)
                for i in range(2)
            ],
        )

    keep, send = prepare(place, block_ids, key_codes, value_codes, value_scales, qkv, prefix, half)
    mate = swap(send, 1)
    queries = (keep, mate)

    pack = jnp.concatenate([keep[:extent], mate[:extent], keep[extent : extent + 8], mate[extent : extent + 8]], axis=0)
    size = pack.shape[0]

    def blocks_of(base, count=1):
        out = []
        for j in range(count):
            b = base + j * size
            out.append((b, b + half * rows, b + 2 * extent))
            out.append((b + extent, b + extent + half * rows, b + 2 * extent + 8))
        return out

    my_books = lax.dynamic_slice_in_dim(codebooks, core * half, half, 0).reshape(half * codes, head_dim)
    own_kv = 2 * half * 2 * tokens
    stretch = jnp.concatenate([keep[-own_kv:], mate[-own_kv:]], axis=0)

    def along(parts, bits):
        return swap(jnp.concatenate(parts, axis=0) if len(parts) > 1 else parts[0], 4 * bits)

    steps = [n_far >> (i + 1) for i in range(n_far.bit_length() - 1)]
    z_one = [along([pack], bits) for bits in steps]
    x_pack = swap(pack, 2)
    y_pack = swap(jnp.concatenate([pack, my_books, stretch], axis=0), 0, 1)
    diag = swap(pack, 2, 1)

    positions = np.arange(rows)
    cos_tok, sin_tok = np.cos(angle_table(positions, head_dim)), np.sin(angle_table(positions, head_dim))
    starts = np.arange(128) * rows
    cos_blk, sin_blk = np.cos(angle_table(starts, head_dim)), np.sin(angle_table(starts, head_dim))
    tables = [jnp.asarray(t.astype(np.float32)) for t in (cos_tok, sin_tok, cos_blk, sin_blk)]
    sizes = (half, rows, groups, tokens, group, head_dim, codes)
    call = functools.partial(attend, place, tables=tables, queries=queries, sizes=sizes)
    own_book = (codebooks, None)

    def pieces(*arrays):
        return [(a, blocks_of(0, a.shape[0] // size)) for a in arrays]

    other_book, other_stretch = (y_pack, size), (y_pack, size + half * codes)

    state = call([(0, own_book, pieces(pack, x_pack, z_one[-1]), False)], stretch=None, state=None, final=False)
    *z_one, first, second, third = lax.optimization_barrier((*z_one, *state))
    state = (first, second, third)
    z_two, reached = [], [z_one[0]]
    for i, bits in enumerate(steps[1:]):
        z_two.append(along(reached, bits))
        reached = reached + [z_one[i + 1], z_two[-1]]
    diag_far = [along([diag], steps[0])]
    near = jnp.concatenate(z_one, axis=0)
    x_near, y_near = swap(near, 2), swap(near, 0, 1)
    state = call(
        [
            (0, own_book, pieces(*z_one[:-1]), True),
            (half, other_book, [(y_pack, blocks_of(0))] + pieces(diag), False),
        ],
        stretch=(*other_stretch, (1,)), state=state, final=False,
    )

    z_rest = jnp.concatenate(z_two, axis=0) if len(z_two) > 1 else z_two[0]
    x_rest, y_rest = swap(z_rest, 2), swap(z_rest, 0, 1)
    diag_far[0], first, second, third = lax.optimization_barrier((diag_far[0], *state))
    state = (first, second, third)
    for bits in steps[1:]:
        diag_far.append(along([diag] + diag_far, bits))
    state = call(
        [
            (0, own_book, pieces(z_rest, x_near), True),
            (half, other_book, pieces(diag_far[0], y_near), True),
        ],
        stretch=(*other_stretch, (0,)), state=state, final=False,
    )
    out, out_send = call(
        [(0, own_book, pieces(x_rest), True), (half, other_book, pieces(*diag_far[1:], y_rest), True)],
        stretch=None, state=state, final=True,
    )
    out_mate = swap(out_send, 1)
    return lay_out(place, out_mate, True, lay_out(place, out, False, None))


def rotate(tensor, position):
    half_dim = tensor.shape[-1] // 2
    ladder = jnp.arange(half_dim, dtype=jnp.float32)
    inverse = jnp.exp(ladder * jnp.float32(-2.0 * math.log(rope_base) / tensor.shape[-1]))
    angles = position.astype(jnp.float32)[:, None] * inverse[None, :]
    target = (position.shape[0],) + (1,) * (tensor.ndim - 2) + (half_dim,)
    cosine = jnp.cos(angles).reshape(target)
    sine_part = jnp.sin(angles).reshape(target)
    floats = tensor.astype(jnp.float32)
    first_half = floats[..., :half_dim]
    second_half = floats[..., half_dim:]
    return jnp.concatenate(
        [
            first_half * cosine - second_half * sine_part,
            second_half * cosine + first_half * sine_part,
        ],
        axis=-1,
    )


def decode_block(key_codes, codebooks):
    block_rows, kv_local, group_count = key_codes.shape
    entries = codebooks.shape[1]
    head_dim = codebooks.shape[2]
    ladder = lax.broadcasted_iota(jnp.int32, (1, 1, 1, entries), 3).astype(jnp.float32)
    one_hot = (key_codes.astype(jnp.float32)[..., None] == ladder).astype(jnp.bfloat16)
    code_table = codebooks.reshape(kv_local, entries, group_count, head_dim // group_count)
    decoded = jnp.einsum("bkgc,kcgd->bkgd", one_hot, code_table, preferred_element_type=jnp.float32)
    return decoded.reshape(block_rows, kv_local, head_dim)


def span_of():
    return 1024


def absorb(state, queries, key_rows, value_rows, allowed):
    running_max, running_sum, weighted = state
    scores = jnp.einsum(
        "tkgd,nkd->tkgn", queries, key_rows, preferred_element_type=jnp.float32
    ) * queries.shape[-1] ** (-0.5)
    if allowed is not None:
        scores = jnp.where(allowed[:, None, None, :], scores, -jnp.inf)
    new_max = jnp.maximum(running_max, jnp.max(scores, axis=-1))
    decay_factor = jnp.exp(running_max - new_max)
    weights = jnp.exp(scores - new_max[..., None])
    running_sum = running_sum * decay_factor + jnp.sum(weights, axis=-1)
    weighted = weighted * decay_factor[..., None] + jnp.einsum(
        "tkgn,nkd->tkgd",
        weights.astype(jnp.bfloat16),
        value_rows,
        preferred_element_type=jnp.float32,
    )
    return (new_max, running_sum, weighted)


def shards(qkv, key_codes, codebooks, value_codes, value_scales, block_ids):
    group_heads = qkv.shape[2] - 2
    head_dim = qkv.shape[3]
    block_rows = key_codes.shape[0]
    prefix_len = block_rows * lax.axis_size("outer")
    prefix_values = (value_codes.astype(jnp.float32) * value_scales[:, :, None]).astype(
        jnp.bfloat16
    )
    exchanged = lax.all_to_all(qkv, "inner", split_axis=1, concat_axis=0, tiled=True)
    stretch_rows = exchanged.shape[0]
    kv_local = exchanged.shape[1]
    local_pos = jnp.arange(stretch_rows, dtype=jnp.int32)
    stretch_pos = prefix_len + local_pos
    queries = rotate(exchanged[:, :, :group_heads, :], stretch_pos).astype(jnp.bfloat16)
    stretch_keys = rotate(exchanged[:, :, group_heads, :], stretch_pos).astype(jnp.bfloat16)
    stretch_values = exchanged[:, :, group_heads + 1, :]
    initial = (
        jnp.full((stretch_rows, kv_local, group_heads), -1e30, jnp.float32),
        jnp.zeros((stretch_rows, kv_local, group_heads), jnp.float32),
        jnp.zeros((stretch_rows, kv_local, group_heads, head_dim), jnp.float32),
    )
    own_pos = block_ids[0] * block_rows + jnp.arange(block_rows, dtype=jnp.int32)
    prefix_keys = rotate(decode_block(key_codes, codebooks), own_pos).astype(jnp.bfloat16)
    key_rows = lax.all_gather(prefix_keys, "outer", axis=0, tiled=True)
    value_rows = lax.all_gather(prefix_values, "outer", axis=0, tiled=True)
    length = key_rows.shape[0]
    span_rows = span_of()

    def advance(step_index, inner_state):
        first_row = step_index * span_rows
        key_part = lax.dynamic_slice_in_dim(key_rows, first_row, span_rows, 0)
        value_part = lax.dynamic_slice_in_dim(value_rows, first_row, span_rows, 0)
        return absorb(inner_state, queries, key_part, value_part, None)

    allowed = local_pos[None, :] <= local_pos[:, None]
    final_state = lax.fori_loop(
        0,
        length // span_rows,
        advance,
        absorb(initial, queries, stretch_keys, stretch_values, allowed),
    )
    running_max, running_sum, weighted = final_state
    outputs = (weighted / running_sum[..., None]).astype(jnp.bfloat16)
    return lax.all_to_all(outputs, "inner", split_axis=0, concat_axis=1, tiled=True)


def solution(mesh):
    n_outer, n_inner = mesh.shape["outer"], mesh.shape["inner"]

    def body(qkv, key_codes, codebooks, value_codes, value_scales, block_ids):
        arrays = (qkv, key_codes, codebooks, value_codes, value_scales, block_ids)
        head_dim = qkv.shape[3]
        far = n_outer // 4
        fits = (
            n_inner == 2
            and n_outer % 4 == 0
            and 4 <= far
            and far & (far - 1) == 0
            and n_outer <= 128
            and key_codes.shape[1] % 2 == 0
            and key_codes.shape[0] == 128
            and head_dim == 128
            and head_dim // key_codes.shape[2] == 8
            and key_codes.shape[2] % 16 == 0
            and codebooks.shape[1] % 128 == 0
            and qkv.shape[2] == 10
            and qkv.shape[0] % 32 == 0
        )
        if fits:
            return paired(*arrays, n_outer=n_outer)
        return shards(*arrays)

    return jax.shard_map(
        body,
        mesh=mesh,
        in_specs=(
            P(("outer", "inner"), None, None, None),
            P("outer", "inner", None),
            P("inner", None, None),
            P("outer", "inner", None),
            P("outer", "inner"),
            P("outer"),
        ),
        out_specs=P(("outer", "inner"), None, None, None),
        check_vma=False,
    )
```
